32 devices in a mesh: member: 8 (over y, x, core), domain: 4 (over z).
Axes of the slice: x: 2, y: 2, z: 4, core: 2. Of those that a mesh axis runs over, the one named last changes fastest.
Arguments:
- state: float32 [8, 4, 128, 512], P('member', None, 'domain'), may hold values from -5 to 5
- perturbation: float32 [8, 4, 128, 512], P('member', None, 'domain'), may hold values from -3 to 3
- parents: int32 [8], replicated, may hold values from 0 to 7
Outputs:
- final_state: float32 [8, 4, 128, 512], P('member', None, 'domain')
- score: float32 [8], P('member')
The draws below stay inside these ranges and needn't reach their ends.
Inputs may be any that keep to these rules, and one draw needn't show every extreme that they name: `parents`: A member may be the parent of several slots or of none.
All inputs are finite; a program needn't handle non-finite values.
Results may differ from the reference program's by a relative error of at most 0.00002.
Values sent between devices are 32-bit elements; how exact they have to be, the bound alone decides.
No kernel may reach another device: no remote copies, remote signals or barrier semaphores. Data moves between devices by JAX's collectives and lax.ppermute only.
A program may use at most 64 MiB of HBM per device.

```python
import math
import jax
import jax.numpy as jnp
import numpy as np
from jax import lax

NLON = 512
STEPS = 3
MEMBERS = 8
NLAT = 128


def set_ends(drawn, own_key, smallest, top_value):
    longest = drawn.shape.index(max(drawn.shape))
    spots = []
    for shift in (0, 1):
        where = [jax.random.randint(jax.random.fold_in(own_key, axis), (), 0, length) for axis, length in enumerate(drawn.shape)]
        where[longest] = (where[longest] + shift) % drawn.shape[longest]
        spots.append(tuple(where))
    return drawn.at[spots[0]].set(smallest).at[spots[1]].set(top_value)


def level_of(key, shape, shards, least, high):
    gain, own = 1.0, jax.random.fold_in(key, 6)
    for axis_at, parts in shards:
        steps = jnp.exp(jax.random.uniform(jax.random.fold_in(own, axis_at), (parts,), jnp.float32, least / len(shards), high / len(shards)))
        gain = gain * jnp.repeat(steps, shape[axis_at] // parts).reshape([-1 if axis == axis_at else 1 for axis in range(len(shape))])
    return gain


def rank_bounds(number_of, skew):
    portions = [(1 << 20) // math.isqrt(standing ** skew) + 1 for standing in range(1, number_of + 1)]
    deviation = 1 + sum(portions) // (1 << 30)
    return np.cumsum(np.array([max(1, weight // deviation) for weight in portions]))


def ranked_ids(stream_key, shape, count, lean):
    grid = rank_bounds(count, lean)
    pick = jax.random.randint(jax.random.fold_in(stream_key, 1), shape, 0, int(grid[count - 1]))
    grade = jnp.searchsorted(jnp.asarray(grid, jnp.int32), pick, side="right")
    return jax.random.permutation(jax.random.fold_in(stream_key, 2), count)[grade].astype(jnp.int32)


def noise(key, shape, deviation, bound, shards=(), kind=jnp.bfloat16):
    result = jax.random.normal(key, shape, jnp.float32) * deviation
    if len(shards) > 0:
        result = level_of(key, shape, shards, -0.22, 0.18) * result
    return jnp.clip(result, min=-bound, max=bound).astype(kind)


def setup_inputs(seed: int = 0) -> dict:
    streams_of = jax.random.split(jax.random.key(seed), 4)
    state = noise(streams_of[0], (MEMBERS, 4, NLAT, NLON), 0.5, 5.0, ((0, 8), (2, 4)), jnp.float32)
    perturbation = noise(streams_of[1], (MEMBERS, 4, NLAT, NLON), 0.3, 3.0, ((0, 8), (2, 4)), jnp.float32)
    parents = set_ends(ranked_ids(streams_of[2], (MEMBERS,), MEMBERS, 2), jax.random.fold_in(streams_of[2], 3), 0, MEMBERS - 1).astype(jnp.int32)
    return dict(state=state, perturbation=perturbation, parents=parents)


time_step = 0.1
viscous = 0.05
coriolis = 1.0


def gradients(padded):
    middle = padded[:, 1:-1]
    east = jnp.roll(middle, -1, axis=-1)
    west = jnp.roll(middle, 1, axis=-1)
    return middle, east, west, padded[:, 2:], padded[:, :-2]


def tendency(padded, start_row, total_rows):
    middle, east, west, north, south = gradients(padded)
    grad_x = (east - west) * 0.5
    grad_y = (north - south) * 0.5
    laplace = east + west + north + south - 4.0 * middle
    depth = 1.0 + padded[0]
    fluxes = jnp.stack([depth * padded[1], depth * padded[2]])
    flux_mid, flux_east, flux_west, flux_north, flux_south = gradients(fluxes)
    count = padded.shape[1] - 2
    global_rows = (start_row + 1 + jnp.arange(count, dtype=jnp.int32)).astype(jnp.float32)
    latitude = coriolis * (2.0 * (global_rows + 0.5) / total_rows - 1.0)
    latitude = latitude[:, None]
    height, speed_u, speed_v, tracer = middle[0], middle[1], middle[2], middle[3]
    advect = speed_u * grad_x + speed_v * grad_y
    d_eta = -((flux_east[0] - flux_west[0]) * 0.5 + (flux_north[1] - flux_south[1]) * 0.5) + viscous * laplace[0]
    d_u = -advect[1] + latitude * speed_v - grad_x[0] + viscous * laplace[1]
    d_v = -advect[2] - latitude * speed_u - grad_y[0] + viscous * laplace[2]
    d_q = -advect[3] + viscous * laplace[3]
    return jnp.stack([d_eta, d_u, d_v, d_q])


def operator(field):
    return tendency(jnp.pad(field, ((0, 0), (1, 1), (0, 0))), -1, NLAT)


def rk_step(field):
    first = field + time_step * operator(field)
    second = 0.75 * field + 0.25 * (first + time_step * operator(first))
    return (1.0 / 3.0) * field + (2.0 / 3.0) * (second + time_step * operator(second))


def run_steps(field):
    for count in range(STEPS):
        field = rk_step(field)
    return field


def reference(state, perturbation, parents):
    before = lax.map(run_steps, state)
    weight = 1.0 + 2.0 * jnp.arange(NLAT, dtype=jnp.int32).astype(jnp.float32) / (NLAT - 1)
    score = jnp.sum(weight[None, :, None] * before[:, 3] * before[:, 3], axis=(1, 2)) / (NLAT * NLON)
    cloned = jnp.take(before, parents, axis=0) + perturbation
    after = lax.map(run_steps, cloned)
    return after, score
```

```python
import functools

import jax
import jax.numpy as jnp
from jax import lax
from jax.experimental import pallas as pl
from jax.experimental.pallas import tpu as pltpu
from jax.sharding import PartitionSpec as P

STEPS = 3
REACH = 3 * STEPS

time_step = 0.1
viscous = 0.05
coriolis = 1.0

LANES = 128
SUB = 8
VMEM = pl.BlockSpec(memory_space=pltpu.VMEM)
SMEM = pl.BlockSpec(memory_space=pltpu.SMEM)


def stage(src, base, dst, first, count, keep, gain, global_row, total_rows):
    chunks = src.shape[1]
    lane = lax.broadcasted_iota(jnp.int32, (SUB, LANES), 1)
    sub = lax.broadcasted_iota(jnp.int32, (SUB, LANES), 0)
    at_last = lane == LANES - 1
    at_first = lane == 0
    step = gain * time_step
    for row in range(first, first + count, SUB):

        def load(field, chunk, offset):
            return src[field, chunk, pl.ds(row + offset, SUB), :]

        cells = [[load(f, j, 0) for j in range(chunks)] for f in range(4)]
        to_west = [[pltpu.roll(c, LANES - 1, 1) for c in line] for line in cells]
        to_east = [[pltpu.roll(c, 1, 1) for c in line] for line in cells]
        rows = (sub + (row + global_row)).astype(jnp.float32)
        turn = ((rows + 0.5) * (2.0 * coriolis / total_rows) - coriolis) * step
        for j in range(chunks):
            c = [cells[f][j] for f in range(4)]
            n = [load(f, j, 1) for f in range(4)]
            s = [load(f, j, -1) for f in range(4)]
            e = [jnp.where(at_last, to_west[f][(j + 1) % chunks], to_west[f][j]) for f in range(4)]
            w = [jnp.where(at_first, to_east[f][(j - 1) % chunks], to_east[f][j]) for f in range(4)]
            dx = [e[f] - w[f] for f in range(4)]
            dy = [n[f] - s[f] for f in range(4)]
            near = [(e[f] + w[f]) + (n[f] + s[f]) for f in range(4)]
            u = c[1] * (-0.5 * step)
            v = c[2] * (-0.5 * step)
            out = [
                near[f] * (step * viscous) + c[f] * (gain - 4.0 * step * viscous)
                for f in range(4)
            ]
            flux = ((1.0 + e[0]) * e[1] - (1.0 + w[0]) * w[1]) + (
                (1.0 + n[0]) * n[2] - (1.0 + s[0]) * s[2]
            )
            out[0] = out[0] + flux * (-0.5 * step)
            out[1] = out[1] + (u * dx[1] + v * dy[1]) + (turn * c[2] - dx[0] * (0.5 * step))
            out[2] = out[2] + (u * dx[2] + v * dy[2]) - (turn * c[1] + dy[0] * (0.5 * step))
            out[3] = out[3] + (u * dx[3] + v * dy[3])
            for f in range(4):
                if keep:
                    out[f] = out[f] + keep * base[f, j, pl.ds(row, SUB), :]
                dst[f, j, pl.ds(row, SUB), :] = out[f]


def advance(bufs, origin, rows, reach, domain, domains, total_rows):
    state, one, two = bufs
    global_row = domain * rows - origin
    thirds = ((state, one, 0.0, 1.0), (one, two, 0.75, 0.25), (two, state, 1.0 / 3.0, 2.0 / 3.0))
    for _ in range(STEPS):
        for src, dst, keep, gain in thirds:
            reach -= 1
            first, count = origin - reach, rows + 2 * reach
            stage(src, state, dst, first, count, keep, gain, global_row, total_rows)
            if reach > 0:
                blank = jnp.zeros(dst.shape[:2] + (1, LANES), jnp.float32)

                @pl.when(domain == 0)
                def _():
                    dst[:, :, pl.ds(origin - 1, 1), :] = blank

                @pl.when(domain == domains - 1)
                def _():
                    dst[:, :, pl.ds(origin + rows, 1), :] = blank


def put(buf, field, row, count, block, row_from, add=False):
    for j in range(buf.shape[1]):
        piece = block[pl.ds(row_from, count), pl.ds(j * LANES, LANES)]
        if add:
            piece = piece + buf[field, j, pl.ds(row, count), :]
        buf[field, j, pl.ds(row, count), :] = piece


class Sizes:
    def __init__(self, rows):
        self.rows = rows
        self.half = rows // 2
        self.extra = max(0, 2 * REACH - self.half)
        self.half_rows = 4 * (self.half + self.extra)
        self.body = REACH // SUB * SUB
        self.tail = REACH - self.body
        self.edge_rows = 8 * REACH

    def half_at(self, field):
        return field * self.half

    def extra_at(self, field):
        return 4 * self.half + field * self.extra

    def edge_at(self, which, field):
        return (which * 4 + field) * self.body

    def tail_at(self, which, field):
        return 8 * self.body + (which * 4 + field) * self.tail


def pack_kernel(sizes, state, pert, mine, other, edge_one, edge_two):
    rows, half, extra, body, tail = sizes.rows, sizes.half, sizes.extra, sizes.body, sizes.tail
    core = lax.rem(lax.axis_index("member"), 2)
    parity = lax.rem(lax.axis_index("domain"), 2)

    def south_half(out):
        for f in range(4):
            out[pl.ds(sizes.half_at(f), half), :] = state[f, pl.ds(0, half), :]
            out[pl.ds(sizes.extra_at(f), extra), :] = state[f, pl.ds(half, extra), :]

    def north_half(out):
        for f in range(4):
            out[pl.ds(sizes.half_at(f), half), :] = state[f, pl.ds(rows - half, half), :]
            out[pl.ds(sizes.extra_at(f), extra), :] = state[f, pl.ds(rows - half - extra, extra), :]

    def south_edge(out):
        for k, a in enumerate((state, pert)):
            for f in range(4):
                out[pl.ds(sizes.edge_at(k, f), body), :] = a[f, pl.ds(0, body), :]
                out[pl.ds(sizes.tail_at(k, f), tail), :] = a[f, pl.ds(body, tail), :]

    def north_edge(out):
        for k, a in enumerate((state, pert)):
            for f in range(4):
                out[pl.ds(sizes.edge_at(k, f), body), :] = a[f, pl.ds(rows - body, body), :]
                out[pl.ds(sizes.tail_at(k, f), tail), :] = a[f, pl.ds(rows - REACH, tail), :]

    @pl.when(core == 0)
    def _():
        south_half(mine)
        north_half(other)

    @pl.when(core == 1)
    def _():
        north_half(mine)
        south_half(other)

    @pl.when(parity == 0)
    def _():
        north_edge(edge_one)
        south_edge(edge_two)

    @pl.when(parity == 1)
    def _():
        south_edge(edge_one)
        north_edge(edge_two)


class Place:
    def __init__(self, chips_a, chips_b):
        self.sizes = (chips_a, chips_b)
        member = lax.axis_index("member")
        self.core = lax.rem(member, 2)
        chip = member // 2
        self.a, self.b = chip // chips_b, lax.rem(chip, chips_b)

    def child(self, hop, core):
        chips_a, chips_b = self.sizes
        a = jnp.where(self.core == 0, lax.rem(self.a + hop, chips_a), self.a)
        b = jnp.where(self.core == 0, self.b, lax.rem(self.b + hop, chips_b))
        return (a * chips_b + b) * 2 + core

    def first_hop(self, parent):
        chips_a, chips_b = self.sizes
        chip = parent // 2
        a, b = chip // chips_b, lax.rem(chip, chips_b)
        return jnp.where(
            self.core == 0,
            lax.rem(self.b - b + chips_b, chips_b),
            lax.rem(self.a - a + chips_a, chips_a),
        )

    def second_hop(self, parent):
        chips_a, chips_b = self.sizes
        chip = parent // 2
        a, b = chip // chips_b, lax.rem(chip, chips_b)
        return jnp.where(
            self.core == 0,
            lax.rem(self.a - a + chips_a, chips_a),
            lax.rem(self.b - b + chips_b, chips_b),
        )


def parent_of(parents, member):
    return jnp.clip(parents[member], 0, parents.shape[0] - 1)


def pick_kernel(chips, hops, parents, *refs):
    place = Place(*chips)
    held, outs = refs[: 2 * hops], refs[2 * hops :]
    at = 0
    for hop in range(hops):
        for own in (True, False):
            core = place.core if own else 1 - place.core
            parent = parent_of(parents, place.child(hop, core))
            index = 2 * place.first_hop(parent) + jnp.where(
                lax.rem(parent, 2) == place.core, 0, 1
            )
            out = outs[at]
            at += 1
            for k in range(2 * hops):

                @pl.when(index == k)
                def _():
                    out[...] = held[k][...]


def settle_kernel(chips, own, parents, *refs):
    place = Place(*chips)
    sources, out = refs[:-1], refs[-1]
    core = place.core if own else 1 - place.core
    parent = parent_of(parents, place.child(0, core))
    index = place.second_hop(parent)
    for k, source in enumerate(sources):

        @pl.when(index == k)
        def _():
            out[...] = source[...]


def put_edges(sizes, which, buf, origin, edge_one, edge_two, add=False):
    rows, body, tail = sizes.rows, sizes.body, sizes.tail
    parity = lax.rem(lax.axis_index("domain"), 2)

    def south(edge):
        for f in range(4):
            put(buf, f, origin - body, body, edge, sizes.edge_at(which, f), add)
            put(buf, f, origin - REACH, tail, edge, sizes.tail_at(which, f), add)

    def north(edge):
        for f in range(4):
            put(buf, f, origin + rows, body, edge, sizes.edge_at(which, f), add)
            put(buf, f, origin + rows + body, tail, edge, sizes.tail_at(which, f), add)

    @pl.when(parity == 0)
    def _():
        north(edge_one)
        south(edge_two)

    @pl.when(parity == 1)
    def _():
        south(edge_one)
        north(edge_two)


def score_kernel(sizes, domains, state, edge_one, edge_two, out, *bufs):
    rows = sizes.rows
    origin = 16
    total_rows = rows * domains
    domain = lax.axis_index("domain")
    for f in range(4):
        put(bufs[0], f, origin, rows, state.at[f], 0)
    put_edges(sizes, 0, bufs[0], origin, edge_one, edge_two)
    advance(bufs, origin, rows, REACH, domain, domains, total_rows)
    sub = lax.broadcasted_iota(jnp.int32, (SUB, LANES), 0)
    total = jnp.zeros((SUB, LANES), jnp.float32)
    for row in range(0, rows, SUB):
        line = jnp.zeros((SUB, LANES), jnp.float32)
        for j in range(bufs[0].shape[1]):
            q = bufs[0][3, j, pl.ds(origin + row, SUB), :]
            line = line + q * q
        place = (sub + (row + domain * rows)).astype(jnp.float32)
        total = total + (1.0 + 2.0 * place / (total_rows - 1)) * line
    out[...] = total


def final_kernel(
    sizes, domains, own_half, far_half, near_halo, far_halo, pert, edge_one, edge_two, out, *bufs
):
    rows, half, extra = sizes.rows, sizes.half, sizes.extra
    origin = 24
    total_rows = rows * domains
    domain = lax.axis_index("domain")
    core = lax.rem(lax.axis_index("member"), 2)
    start = bufs[0]

    def fill(south, north, south_halo, north_halo):
        for f in range(4):
            at, more = sizes.half_at(f), sizes.extra_at(f)
            put(start, f, origin - half, half, south_halo, at)
            put(start, f, origin - half - extra, extra, south_halo, more)
            put(start, f, origin, half, south, at)
            put(start, f, origin + half, half, north, at)
            put(start, f, origin + rows, half, north_halo, at)
            put(start, f, origin + rows + half, extra, north_halo, more)

    @pl.when(core == 0)
    def _():
        fill(own_half, far_half, near_halo, far_halo)

    @pl.when(core == 1)
    def _():
        fill(far_half, own_half, far_halo, near_halo)

    advance(bufs, origin, rows, 2 * REACH, domain, domains, total_rows)
    for f in range(4):
        put(start, f, origin, rows, pert.at[f], 0, add=True)
    put_edges(sizes, 1, start, origin, edge_one, edge_two, add=True)
    advance(bufs, origin, rows, REACH, domain, domains, total_rows)
    for f in range(4):
        for j in range(start.shape[1]):
            out[f, :, pl.ds(j * LANES, LANES)] = start[f, j, pl.ds(origin, rows), :]


def chip_grid(chips):
    b = 1
    while chips % (2 * b) == 0 and (2 * b) * (2 * b) <= chips:
        b *= 2
    return chips // b, b


def on_device(state, perturbation, parents, members, domains):
    state, perturbation = state[0], perturbation[0]
    rows, width = state.shape[1:]
    sizes = Sizes(rows)
    chunks = width // LANES
    chips = chip_grid(members // 2)
    chips_a, chips_b = chips
    hops = max(chips)
    params = pltpu.CompilerParams(vmem_limit_bytes=40 * 2**20)
    half_shape = jax.ShapeDtypeStruct((sizes.half_rows, width), jnp.float32)
    edge_shape = jax.ShapeDtypeStruct((sizes.edge_rows, width), jnp.float32)

    def member(a, b, core):
        return ((a % chips_a) * chips_b + b % chips_b) * 2 + core

    everywhere = [(a, b) for a in range(chips_a) for b in range(chips_b)]
    sibling = [(i, i ^ 1) for i in range(members)]

    def same_core(first, k):
        pairs = []
        for a, b in everywhere:
            if k < (chips_b if first else chips_a):
                pairs.append((member(a, b, 0), member(a, b + k, 0) if first else member(a + k, b, 0)))
            if k < (chips_a if first else chips_b):
                pairs.append((member(a, b, 1), member(a + k, b, 1) if first else member(a, b + k, 1)))
        return pairs

    def other_core(k):
        pairs = []
        for a, b in everywhere:
            if k < chips_a:
                pairs.append((member(a, b, 0), member(a + k, b, 1)))
            if k < chips_b:
                pairs.append((member(a, b, 1), member(a, b + k, 0)))
        return pairs

    def flat(m, z):
        return m * domains + z

    south_north = []
    for chip in range(members // 2):
        for z in range(1, domains):
            south_north.append((flat(2 * chip, z), flat(2 * chip + 1, z - 1)))
            south_north.append((flat(2 * chip + 1, z - 1), flat(2 * chip, z)))
    both = ("member", "domain")
    pair_one = [(z, z ^ 1) for z in range(domains) if z ^ 1 < domains]
    pair_two = [(z, ((z + 1) ^ 1) - 1) for z in range(domains) if 0 <= ((z + 1) ^ 1) - 1 < domains]

    mine, other, edge_one, edge_two = pl.pallas_call(
        functools.partial(pack_kernel, sizes),
        out_shape=(half_shape, half_shape, edge_shape, edge_shape),
        in_specs=[VMEM, VMEM],
        out_specs=(VMEM,) * 4,
        compiler_params=params,
    )(state, perturbation)

    held = [mine, None]
    for k in range(1, hops):
        held.append(lax.ppermute(mine, "member", same_core(True, k)))
        held.append(lax.ppermute(other, "member", other_core(k)))
    held[1] = lax.ppermute(other, "member", sibling)
    edge_one = lax.ppermute(edge_one, "domain", pair_one)
    edge_two = lax.ppermute(edge_two, "domain", pair_two)

    picked = pl.pallas_call(
        functools.partial(pick_kernel, chips, hops),
        out_shape=(half_shape,) * (2 * hops),
        in_specs=[SMEM] + [VMEM] * (2 * hops),
        out_specs=(VMEM,) * (2 * hops),
        compiler_params=params,
    )(parents, *held)

    def settle(own):
        which = 0 if own else 1
        sources = [picked[which]]
        for k in range(1, hops):
            sources.append(lax.ppermute(picked[2 * k + which], "member", same_core(False, k)))
        return pl.pallas_call(
            functools.partial(settle_kernel, chips, own),
            out_shape=half_shape,
            in_specs=[SMEM] + [VMEM] * hops,
            out_specs=VMEM,
            compiler_params=params,
        )(parents, *sources)

    own_half = settle(True)
    sibling_halo = lax.ppermute(own_half, both, south_north)
    sibling_half = settle(False)
    near_halo = lax.ppermute(sibling_half, both, south_north)
    far_half = lax.ppermute(sibling_half, "member", sibling)
    far_halo = lax.ppermute(sibling_halo, "member", sibling)

    score = pl.pallas_call(
        functools.partial(score_kernel, sizes, domains),
        out_shape=jax.ShapeDtypeStruct((SUB, LANES), jnp.float32),
        in_specs=[VMEM] * 3,
        out_specs=VMEM,
        scratch_shapes=[pltpu.VMEM((4, chunks, rows + 32, LANES), jnp.float32)] * 3,
        compiler_params=params,
    )(state, edge_one, edge_two)
    if domains & (domains - 1) == 0:
        bit = 1
        while bit < domains:
            score = score + lax.ppermute(score, "domain", [(z, z ^ bit) for z in range(domains)])
            bit *= 2
    else:
        score = lax.psum(score, "domain")
    score = jnp.sum(score) / (rows * domains * width)

    after = pl.pallas_call(
        functools.partial(final_kernel, sizes, domains),
        out_shape=jax.ShapeDtypeStruct((4, rows, width), jnp.float32),
        in_specs=[VMEM] * 7,
        out_specs=VMEM,
        scratch_shapes=[pltpu.VMEM((4, chunks, rows + 48, LANES), jnp.float32)] * 3,
        compiler_params=params,
    )(own_half, far_half, near_halo, far_halo, perturbation, edge_one, edge_two)
    return after[None], jnp.reshape(score, (1,))


def solution(mesh):
    placed = (P("member", None, "domain", None), P("member", None, "domain", None), P())
    return jax.shard_map(
        functools.partial(
            on_device, members=mesh.shape["member"], domains=mesh.shape["domain"]
        ),
        mesh=mesh,
        in_specs=placed,
        out_specs=(P("member", None, "domain", None), P("member")),
        check_vma=False,
    )
```

```python
import functools

import jax
import jax.numpy as jnp
from jax import lax
from jax.experimental import pallas as pl
from jax.experimental.pallas import tpu as pltpu
from jax.sharding import PartitionSpec as P

STEPS = 3
REACH = 3 * STEPS

time_step = 0.1
viscous = 0.05
coriolis = 1.0

LANES = 128
SUB = 8
VMEM = pl.BlockSpec(memory_space=pltpu.VMEM)
SMEM = pl.BlockSpec(memory_space=pltpu.SMEM)


def stage(src, base, dst, first, count, keep, gain, global_row, total_rows):
    chunks = src.shape[1]
    lane = lax.broadcasted_iota(jnp.int32, (SUB, LANES), 1)
    sub = lax.broadcasted_iota(jnp.int32, (SUB, LANES), 0)
    at_last = lane == LANES - 1
    at_first = lane == 0
    step = gain * time_step
    for row in range(first, first + count, SUB):

        def load(field, chunk, offset):
            return src[field, chunk, pl.ds(row + offset, SUB), :]

        cells = [[load(f, j, 0) for j in range(chunks)] for f in range(4)]
        to_west = [[pltpu.roll(c, LANES - 1, 1) for c in line] for line in cells]
        to_east = [[pltpu.roll(c, 1, 1) for c in line] for line in cells]
        rows = (sub + (row + global_row)).astype(jnp.float32)
        turn = ((rows + 0.5) * (2.0 * coriolis / total_rows) - coriolis) * step
        for j in range(chunks):
            c = [cells[f][j] for f in range(4)]
            n = [load(f, j, 1) for f in range(4)]
            s = [load(f, j, -1) for f in range(4)]
            e = [jnp.where(at_last, to_west[f][(j + 1) % chunks], to_west[f][j]) for f in range(4)]
            w = [jnp.where(at_first, to_east[f][(j - 1) % chunks], to_east[f][j]) for f in range(4)]
            dx = [e[f] - w[f] for f in range(4)]
            dy = [n[f] - s[f] for f in range(4)]
            near = [(e[f] + w[f]) + (n[f] + s[f]) for f in range(4)]
            u = c[1] * (-0.5 * step)
            v = c[2] * (-0.5 * step)
            out = [
                near[f] * (step * viscous) + c[f] * (gain - 4.0 * step * viscous)
                for f in range(4)
            ]
            flux = ((1.0 + e[0]) * e[1] - (1.0 + w[0]) * w[1]) + (
                (1.0 + n[0]) * n[2] - (1.0 + s[0]) * s[2]
            )
            out[0] = out[0] + flux * (-0.5 * step)
            out[1] = out[1] + (u * dx[1] + v * dy[1]) + (turn * c[2] - dx[0] * (0.5 * step))
            out[2] = out[2] + (u * dx[2] + v * dy[2]) - (turn * c[1] + dy[0] * (0.5 * step))
            out[3] = out[3] + (u * dx[3] + v * dy[3])
            for f in range(4):
                if keep:
                    out[f] = out[f] + keep * base[f, j, pl.ds(row, SUB), :]
                dst[f, j, pl.ds(row, SUB), :] = out[f]


def advance(bufs, origin, rows, reach, domain, domains, total_rows):
    state, one, two = bufs
    global_row = domain * rows - origin
    thirds = ((state, one, 0.0, 1.0), (one, two, 0.75, 0.25), (two, state, 1.0 / 3.0, 2.0 / 3.0))
    for _ in range(STEPS):
        for src, dst, keep, gain in thirds:
            reach -= 1
            first, count = origin - reach, rows + 2 * reach
            stage(src, state, dst, first, count, keep, gain, global_row, total_rows)
            if reach > 0:
                blank = jnp.zeros(dst.shape[:2] + (1, LANES), jnp.float32)

                @pl.when(domain == 0)
                def _():
                    dst[:, :, pl.ds(origin - 1, 1), :] = blank

                @pl.when(domain == domains - 1)
                def _():
                    dst[:, :, pl.ds(origin + rows, 1), :] = blank


def put(buf, field, row, count, block, row_from, add=False):
    for j in range(buf.shape[1]):
        piece = block[pl.ds(row_from, count), pl.ds(j * LANES, LANES)]
        if add:
            piece = piece + buf[field, j, pl.ds(row, count), :]
        buf[field, j, pl.ds(row, count), :] = piece


class Sizes:
    def __init__(self, rows):
        self.rows = rows
        self.half = rows // 2
        self.half_rows = 4 * self.half
        self.body = REACH // SUB * SUB
        self.tail = REACH - self.body
        self.edge_rows = -(-4 * REACH // SUB) * SUB

    def half_at(self, field):
        return field * self.half

    def edge_at(self, field):
        return field * self.body

    def tail_at(self, field):
        return 4 * self.body + field * self.tail


def south_edge(sizes, load, out):
    for f in range(4):
        out[pl.ds(sizes.edge_at(f), sizes.body), :] = load(f, 0, sizes.body)
        out[pl.ds(sizes.tail_at(f), sizes.tail), :] = load(f, sizes.body, sizes.tail)


def north_edge(sizes, load, out, rows):
    for f in range(4):
        out[pl.ds(sizes.edge_at(f), sizes.body), :] = load(f, rows - sizes.body, sizes.body)
        out[pl.ds(sizes.tail_at(f), sizes.tail), :] = load(f, rows - REACH, sizes.tail)


def edges_kernel(sizes, state, edge_one, edge_two):
    parity = lax.rem(lax.axis_index("domain"), 2)

    def load(f, row, count):
        return state[f, pl.ds(row, count), :]

    @pl.when(parity == 0)
    def _():
        north_edge(sizes, load, edge_one, sizes.rows)
        south_edge(sizes, load, edge_two)

    @pl.when(parity == 1)
    def _():
        south_edge(sizes, load, edge_one)
        north_edge(sizes, load, edge_two, sizes.rows)


class Place:
    def __init__(self, chips_a, chips_b):
        self.sizes = (chips_a, chips_b)
        member = lax.axis_index("member")
        self.core = lax.rem(member, 2)
        chip = member // 2
        self.a, self.b = chip // chips_b, lax.rem(chip, chips_b)

    def child(self, hop, core):
        chips_a, chips_b = self.sizes
        a = jnp.where(self.core == 0, lax.rem(self.a + hop, chips_a), self.a)
        b = jnp.where(self.core == 0, self.b, lax.rem(self.b + hop, chips_b))
        return (a * chips_b + b) * 2 + core

    def first_hop(self, parent):
        chips_a, chips_b = self.sizes
        chip = parent // 2
        a, b = chip // chips_b, lax.rem(chip, chips_b)
        return jnp.where(
            self.core == 0,
            lax.rem(self.b - b + chips_b, chips_b),
            lax.rem(self.a - a + chips_a, chips_a),
        )

    def second_hop(self, parent):
        chips_a, chips_b = self.sizes
        chip = parent // 2
        a, b = chip // chips_b, lax.rem(chip, chips_b)
        return jnp.where(
            self.core == 0,
            lax.rem(self.a - a + chips_a, chips_a),
            lax.rem(self.b - b + chips_b, chips_b),
        )


def parent_of(parents, member):
    return jnp.clip(parents[member], 0, parents.shape[0] - 1)


def routes_kernel(chips, hops, parents, out):
    place = Place(*chips)
    tile = 0
    for hop in range(hops):
        for own in (True, False):
            core = place.core if own else 1 - place.core
            parent = parent_of(parents, place.child(hop, core))
            same = jnp.where(lax.rem(parent, 2) == place.core, 0, 1)
            index = 2 * place.first_hop(parent) + same
            out[pl.ds(tile * SUB, SUB), :] = jnp.full((SUB, LANES), index, jnp.int32)
            tile += 1
    for own in (True, False):
        core = place.core if own else 1 - place.core
        index = place.second_hop(parent_of(parents, place.child(0, core)))
        out[pl.ds(tile * SUB, SUB), :] = jnp.full((SUB, LANES), index, jnp.int32)
        tile += 1


def choose(routes, tile, sources, out):
    index = routes[pl.ds(tile * SUB, SUB), :]
    takes = [index == k for k in range(1, len(sources))]
    for row in range(0, out.shape[0], SUB):
        for lane in range(0, out.shape[1], LANES):
            where = (pl.ds(row, SUB), pl.ds(lane, LANES))
            value = sources[0][where]
            for take, source in zip(takes, sources[1:]):
                value = jnp.where(take, source[where], value)
            out[where] = value


def pick_kernel(hops, routes, *refs):
    held, outs = refs[: 2 * hops], refs[-2 * hops :]
    for tile, out in enumerate(outs):
        choose(routes, tile, held, out)


def settle_kernel(sizes, hops, routes, pert, sibling_pert, *refs):
    own_half, sibling_half, own_edge, sibling_edge = refs[-4:]
    core = lax.rem(lax.axis_index("member"), 2)
    for own, out, added in ((0, own_half, pert), (1, sibling_half, sibling_pert)):
        choose(routes, 2 * hops + own, refs[own * hops : (own + 1) * hops], out)
        for f in range(4):
            first = pl.multiple_of(core * sizes.half, SUB)
            at = pl.ds(sizes.half_at(f), sizes.half)
            out[at, :] = out[at, :] + added[f, pl.ds(first, sizes.half), :]
    for half, edge in ((own_half, own_edge), (sibling_half, sibling_edge)):

        def load(f, row, count):
            return half[pl.ds(sizes.half_at(f) + row, count), :]

        @pl.when(core == 0)
        def _():
            south_edge(sizes, load, edge)

        @pl.when(core == 1)
        def _():
            north_edge(sizes, load, edge, sizes.half)


ORIGIN = 16


def put_south(sizes, buf, edge):
    for f in range(4):
        put(buf, f, ORIGIN - sizes.body, sizes.body, edge, sizes.edge_at(f))
        put(buf, f, ORIGIN - REACH, sizes.tail, edge, sizes.tail_at(f))


def put_north(sizes, buf, edge):
    for f in range(4):
        put(buf, f, ORIGIN + sizes.rows, sizes.body, edge, sizes.edge_at(f))
        put(buf, f, ORIGIN + sizes.rows + sizes.body, sizes.tail, edge, sizes.tail_at(f))


def before_kernel(sizes, domains, state, edge_one, edge_two, mine, other, score, *bufs):
    rows, half = sizes.rows, sizes.half
    total_rows = rows * domains
    domain = lax.axis_index("domain")
    parity = lax.rem(domain, 2)
    core = lax.rem(lax.axis_index("member"), 2)
    start = bufs[0]
    chunks = start.shape[1]
    for f in range(4):
        put(start, f, ORIGIN, rows, state.at[f], 0)

    @pl.when(parity == 0)
    def _():
        put_north(sizes, start, edge_one)
        put_south(sizes, start, edge_two)

    @pl.when(parity == 1)
    def _():
        put_south(sizes, start, edge_one)
        put_north(sizes, start, edge_two)

    advance(bufs, ORIGIN, rows, REACH, domain, domains, total_rows)
    for f in range(4):
        for j in range(chunks):
            at = (pl.ds(sizes.half_at(f), half), pl.ds(j * LANES, LANES))
            first = pl.multiple_of(ORIGIN + core * half, SUB)
            mine[at] = start[f, j, pl.ds(first, half), :]
            first = pl.multiple_of(ORIGIN + (1 - core) * half, SUB)
            other[at] = start[f, j, pl.ds(first, half), :]
    sub = lax.broadcasted_iota(jnp.int32, (SUB, LANES), 0)
    total = jnp.zeros((SUB, LANES), jnp.float32)
    for row in range(0, rows, SUB):
        line = jnp.zeros((SUB, LANES), jnp.float32)
        for j in range(chunks):
            q = start[3, j, pl.ds(ORIGIN + row, SUB), :]
            line = line + q * q
        place = (sub + (row + domain * rows)).astype(jnp.float32)
        total = total + (1.0 + 2.0 * place / (total_rows - 1)) * line
    score[...] = total


def after_kernel(
    sizes, domains, own_half, far_half, near_halo, far_halo, score_one, score_two, out, score, *bufs
):
    rows, half = sizes.rows, sizes.half
    total_rows = rows * domains
    domain = lax.axis_index("domain")
    core = lax.rem(lax.axis_index("member"), 2)
    start = bufs[0]
    chunks = start.shape[1]
    score[0, 0] = jnp.sum(score_one[...] + score_two[...]) / (total_rows * out.shape[2])
    for f in range(4):
        at = sizes.half_at(f)
        put(start, f, pl.multiple_of(ORIGIN + core * half, SUB), half, own_half, at)
        put(start, f, pl.multiple_of(ORIGIN + (1 - core) * half, SUB), half, far_half, at)

    @pl.when(core == 0)
    def _():
        put_south(sizes, start, near_halo)
        put_north(sizes, start, far_halo)

    @pl.when(core == 1)
    def _():
        put_south(sizes, start, far_halo)
        put_north(sizes, start, near_halo)

    advance(bufs, ORIGIN, rows, REACH, domain, domains, total_rows)
    for f in range(4):
        for j in range(chunks):
            out[f, :, pl.ds(j * LANES, LANES)] = start[f, j, pl.ds(ORIGIN, rows), :]


def chip_grid(chips):
    b = 1
    while chips % (2 * b) == 0 and (2 * b) * (2 * b) <= chips:
        b *= 2
    return chips // b, b


def on_device(state, perturbation, parents, members, domains):
    state, perturbation = state[0], perturbation[0]
    rows, width = state.shape[1:]
    sizes = Sizes(rows)
    chunks = width // LANES
    chips = chip_grid(members // 2)
    chips_a, chips_b = chips
    hops = max(chips)
    params = pltpu.CompilerParams(vmem_limit_bytes=40 * 2**20)
    half_shape = jax.ShapeDtypeStruct((sizes.half_rows, width), jnp.float32)
    score_shape = jax.ShapeDtypeStruct((SUB, LANES), jnp.float32)
    edge_shape = jax.ShapeDtypeStruct((sizes.edge_rows, width), jnp.float32)

    def member(a, b, core):
        return ((a % chips_a) * chips_b + b % chips_b) * 2 + core

    everywhere = [(a, b) for a in range(chips_a) for b in range(chips_b)]
    sibling = [(i, i ^ 1) for i in range(members)]

    def same_core(first, k):
        pairs = []
        for a, b in everywhere:
            if k < (chips_b if first else chips_a):
                pairs.append((member(a, b, 0), member(a, b + k, 0) if first else member(a + k, b, 0)))
            if k < (chips_a if first else chips_b):
                pairs.append((member(a, b, 1), member(a + k, b, 1) if first else member(a, b + k, 1)))
        return pairs

    def other_core(k):
        pairs = []
        for a, b in everywhere:
            if k < chips_a:
                pairs.append((member(a, b, 0), member(a + k, b, 1)))
            if k < chips_b:
                pairs.append((member(a, b, 1), member(a, b + k, 0)))
        return pairs

    def flat(m, z):
        return m * domains + z

    to_other, to_same = [], []
    for chip in range(members // 2):
        for z in range(1, domains):
            for target, way in ((1, to_other), (0, to_same)):
                way.append((flat(2 * chip, z), flat(2 * chip + target, z - 1)))
            for target, way in ((0, to_other), (1, to_same)):
                way.append((flat(2 * chip + 1, z - 1), flat(2 * chip + target, z)))
    both = ("member", "domain")
    pair_one = [(z, z ^ 1) for z in range(domains) if z ^ 1 < domains]
    pair_two = [(z, ((z + 1) ^ 1) - 1) for z in range(domains) if 0 <= ((z + 1) ^ 1) - 1 < domains]

    def call(kernel, out_shape, in_specs, out_specs, scratch=()):
        return pl.pallas_call(
            kernel,
            out_shape=out_shape,
            in_specs=in_specs,
            out_specs=out_specs,
            scratch_shapes=scratch,
            compiler_params=params,
        )

    bufs = [pltpu.VMEM((4, chunks, rows + 32, LANES), jnp.float32)] * 3
    edge_one, edge_two = call(
        functools.partial(edges_kernel, sizes), (edge_shape,) * 2, [VMEM], (VMEM,) * 2
    )(state)
    edge_one = lax.ppermute(edge_one, "domain", pair_one)
    edge_two = lax.ppermute(edge_two, "domain", pair_two)
    sibling_pert = lax.ppermute(perturbation, "member", sibling)
    routes = call(
        functools.partial(routes_kernel, chips, hops),
        jax.ShapeDtypeStruct(((2 * hops + 2) * SUB, LANES), jnp.int32),
        [SMEM],
        VMEM,
    )(parents)

    mine, other, score = call(
        functools.partial(before_kernel, sizes, domains),
        (half_shape, half_shape, score_shape),
        [VMEM] * 3,
        (VMEM,) * 3,
        bufs,
    )(state, edge_one, edge_two)

    held = [mine, lax.ppermute(other, "member", sibling)]
    for k in range(1, hops):
        held.append(lax.ppermute(mine, "member", same_core(True, k)))
        held.append(lax.ppermute(other, "member", other_core(k)))

    scores = [score, jnp.zeros_like(score)]
    if domains & (domains - 1) == 0:
        bit = 1
        while bit < domains:
            score = scores[0] if bit == 1 else scores[0] + scores[1]
            pairs = [(z, z ^ bit) for z in range(domains)]
            scores = [score, lax.ppermute(score, "domain", pairs)]
            bit *= 2
    else:
        scores[0] = lax.psum(score, "domain")

    picked = call(
        functools.partial(pick_kernel, hops),
        (half_shape,) * (2 * hops),
        [VMEM] * (2 * hops + 2),
        (VMEM,) * (2 * hops),
    )(routes, *held, scores[0])

    own, other = [picked[0]], [picked[1]]
    for k in range(1, hops):
        own.append(lax.ppermute(picked[2 * k], "member", same_core(False, k)))
        other.append(lax.ppermute(picked[2 * k + 1], "member", same_core(False, k)))
    own_half, sibling_half, own_edge, sibling_edge = call(
        functools.partial(settle_kernel, sizes, hops),
        (half_shape, half_shape, edge_shape, edge_shape),
        [VMEM] * (2 * hops + 4),
        (VMEM,) * 4,
    )(routes, perturbation, sibling_pert, *own, *other, scores[1])
    near_halo = lax.ppermute(sibling_edge, both, to_other)
    far_halo = lax.ppermute(own_edge, both, to_same)
    far_half = lax.ppermute(sibling_half, "member", sibling)

    after, score = call(
        functools.partial(after_kernel, sizes, domains),
        (
            jax.ShapeDtypeStruct((4, rows, width), jnp.float32),
            jax.ShapeDtypeStruct((1, 1), jnp.float32),
        ),
        [VMEM] * 6,
        (VMEM, SMEM),
        bufs,
    )(own_half, far_half, near_halo, far_halo, *scores)
    return after[None], jnp.reshape(score, (1,))


def solution(mesh):
    placed = (P("member", None, "domain", None), P("member", None, "domain", None), P())
    return jax.shard_map(
        functools.partial(
            on_device, members=mesh.shape["member"], domains=mesh.shape["domain"]
        ),
        mesh=mesh,
        in_specs=placed,
        out_specs=(P("member", None, "domain", None), P("member")),
        check_vma=False,
    )
```

```python
import functools

import jax
import jax.numpy as jnp
from jax import lax
from jax.experimental import pallas as pl
from jax.experimental.pallas import tpu as pltpu
from jax.sharding import PartitionSpec as P

STEPS = 3
REACH = 3 * STEPS

time_step = 0.1
viscous = 0.05
coriolis = 1.0

LANES = 128
SUB = 8
VMEM = pl.BlockSpec(memory_space=pltpu.VMEM)
SMEM = pl.BlockSpec(memory_space=pltpu.SMEM)


def stage(src, base, dst, first, count, keep, gain, global_row, total_rows):
    chunks = src.shape[1]
    lane = lax.broadcasted_iota(jnp.int32, (SUB, LANES), 1)
    sub = lax.broadcasted_iota(jnp.int32, (SUB, LANES), 0)
    at_last = lane == LANES - 1
    at_first = lane == 0
    step = gain * time_step
    for row in range(first, first + count, SUB):

        def load(field, chunk, offset):
            return src[field, chunk, pl.ds(row + offset, SUB), :]

        cells = [[load(f, j, 0) for j in range(chunks)] for f in range(4)]
        to_west = [[pltpu.roll(c, LANES - 1, 1) for c in line] for line in cells]
        to_east = [[pltpu.roll(c, 1, 1) for c in line] for line in cells]
        rows = (sub + (row + global_row)).astype(jnp.float32)
        turn = ((rows + 0.5) * (2.0 * coriolis / total_rows) - coriolis) * step
        for j in range(chunks):
            c = [cells[f][j] for f in range(4)]
            n = [load(f, j, 1) for f in range(4)]
            s = [load(f, j, -1) for f in range(4)]
            e = [jnp.where(at_last, to_west[f][(j + 1) % chunks], to_west[f][j]) for f in range(4)]
            w = [jnp.where(at_first, to_east[f][(j - 1) % chunks], to_east[f][j]) for f in range(4)]
            dx = [e[f] - w[f] for f in range(4)]
            dy = [n[f] - s[f] for f in range(4)]
            near = [(e[f] + w[f]) + (n[f] + s[f]) for f in range(4)]
            u = c[1] * (-0.5 * step)
            v = c[2] * (-0.5 * step)
            out = [
                near[f] * (step * viscous) + c[f] * (gain - 4.0 * step * viscous)
                for f in range(4)
            ]
            flux = ((1.0 + e[0]) * e[1] - (1.0 + w[0]) * w[1]) + (
                (1.0 + n[0]) * n[2] - (1.0 + s[0]) * s[2]
            )
            out[0] = out[0] + flux * (-0.5 * step)
            out[1] = out[1] + (u * dx[1] + v * dy[1]) + (turn * c[2] - dx[0] * (0.5 * step))
            out[2] = out[2] + (u * dx[2] + v * dy[2]) - (turn * c[1] + dy[0] * (0.5 * step))
            out[3] = out[3] + (u * dx[3] + v * dy[3])
            for f in range(4):
                if keep:
                    out[f] = out[f] + keep * base[f, j, pl.ds(row, SUB), :]
                dst[f, j, pl.ds(row, SUB), :] = out[f]


def advance(bufs, origin, rows, reach, domain, domains, total_rows):
    state, one, two = bufs
    global_row = domain * rows - origin
    blank = jnp.zeros(state.shape[:2] + (1, LANES), jnp.float32)

    def blank_outside(buf):
        @pl.when(domain == 0)
        def _():
            buf[:, :, pl.ds(origin - 1, 1), :] = blank

        @pl.when(domain == domains - 1)
        def _():
            buf[:, :, pl.ds(origin + rows, 1), :] = blank

    blank_outside(state)
    thirds = ((state, one, 0.0, 1.0), (one, two, 0.75, 0.25), (two, state, 1.0 / 3.0, 2.0 / 3.0))
    for _ in range(STEPS):
        for src, dst, keep, gain in thirds:
            reach -= 1
            first, count = origin - reach, rows + 2 * reach
            stage(src, state, dst, first, count, keep, gain, global_row, total_rows)
            if reach > 0:
                blank_outside(dst)


def put(buf, field, row, count, block, row_from, add=False):
    for j in range(buf.shape[1]):
        piece = block[pl.ds(row_from, count), pl.ds(j * LANES, LANES)]
        if add:
            piece = piece + buf[field, j, pl.ds(row, count), :]
        buf[field, j, pl.ds(row, count), :] = piece


class Sizes:
    def __init__(self, rows):
        self.rows = rows
        self.half = rows // 2
        self.half_rows = 4 * self.half
        self.body = REACH // SUB * SUB
        self.tail = REACH - self.body
        self.edge_rows = -(-4 * REACH // SUB) * SUB

    def half_at(self, field):
        return field * self.half

    def edge_at(self, field):
        return field * self.body

    def tail_at(self, field):
        return 4 * self.body + field * self.tail


def south_edge(sizes, load, out):
    for f in range(4):
        out[pl.ds(sizes.edge_at(f), sizes.body), :] = load(f, 0, sizes.body)
        out[pl.ds(sizes.tail_at(f), sizes.tail), :] = load(f, sizes.body, sizes.tail)


def north_edge(sizes, load, out, rows):
    for f in range(4):
        out[pl.ds(sizes.edge_at(f), sizes.body), :] = load(f, rows - sizes.body, sizes.body)
        out[pl.ds(sizes.tail_at(f), sizes.tail), :] = load(f, rows - REACH, sizes.tail)


def edges_kernel(sizes, state, edge_one, edge_two):
    parity = lax.rem(lax.axis_index("domain"), 2)

    def load(f, row, count):
        return state[f, pl.ds(row, count), :]

    @pl.when(parity == 0)
    def _():
        north_edge(sizes, load, edge_one, sizes.rows)
        south_edge(sizes, load, edge_two)

    @pl.when(parity == 1)
    def _():
        south_edge(sizes, load, edge_one)
        north_edge(sizes, load, edge_two, sizes.rows)


class Place:
    def __init__(self, chips_a, chips_b):
        self.sizes = (chips_a, chips_b)
        member = lax.axis_index("member")
        self.core = lax.rem(member, 2)
        chip = member // 2
        self.a, self.b = chip // chips_b, lax.rem(chip, chips_b)

    def child(self, hop, core):
        chips_a, chips_b = self.sizes
        a = jnp.where(self.core == 0, lax.rem(self.a + hop, chips_a), self.a)
        b = jnp.where(self.core == 0, self.b, lax.rem(self.b + hop, chips_b))
        return (a * chips_b + b) * 2 + core

    def first_hop(self, parent):
        chips_a, chips_b = self.sizes
        chip = parent // 2
        a, b = chip // chips_b, lax.rem(chip, chips_b)
        return jnp.where(
            self.core == 0,
            lax.rem(self.b - b + chips_b, chips_b),
            lax.rem(self.a - a + chips_a, chips_a),
        )

    def second_hop(self, parent):
        chips_a, chips_b = self.sizes
        chip = parent // 2
        a, b = chip // chips_b, lax.rem(chip, chips_b)
        return jnp.where(
            self.core == 0,
            lax.rem(self.a - a + chips_a, chips_a),
            lax.rem(self.b - b + chips_b, chips_b),
        )


def parent_of(parents, member):
    return jnp.clip(parents[member], 0, parents.shape[0] - 1)


def routes_kernel(chips, hops, parents, out):
    place = Place(*chips)
    tile = 0
    for hop in range(hops):
        for own in (True, False):
            core = place.core if own else 1 - place.core
            parent = parent_of(parents, place.child(hop, core))
            same = jnp.where(lax.rem(parent, 2) == place.core, 0, 1)
            index = 2 * place.first_hop(parent) + same
            out[pl.ds(tile * SUB, SUB), :] = jnp.full((SUB, LANES), index, jnp.int32)
            tile += 1
    for own in (True, False):
        core = place.core if own else 1 - place.core
        index = place.second_hop(parent_of(parents, place.child(0, core)))
        out[pl.ds(tile * SUB, SUB), :] = jnp.full((SUB, LANES), index, jnp.int32)
        tile += 1


def choose(routes, tile, sources, out):
    index = routes[pl.ds(tile * SUB, SUB), :]
    takes = [index == k for k in range(1, len(sources))]
    for row in range(0, out.shape[0], SUB):
        for lane in range(0, out.shape[1], LANES):
            where = (pl.ds(row, SUB), pl.ds(lane, LANES))
            value = sources[0][where]
            for take, source in zip(takes, sources[1:]):
                value = jnp.where(take, source[where], value)
            out[where] = value


def pick_kernel(hops, routes, *refs):
    held, outs = refs[: 2 * hops], refs[-2 * hops :]
    for tile, out in enumerate(outs):
        choose(routes, tile, held, out)


def settle_kernel(sizes, hops, routes, pert, sibling_pert, *refs):
    own_half, sibling_half, own_edge, sibling_edge = refs[-4:]
    core = lax.rem(lax.axis_index("member"), 2)
    for own, out, added in ((0, own_half, pert), (1, sibling_half, sibling_pert)):
        choose(routes, 2 * hops + own, refs[own * hops : (own + 1) * hops], out)
        for f in range(4):
            first = pl.multiple_of(core * sizes.half, SUB)
            at = pl.ds(sizes.half_at(f), sizes.half)
            out[at, :] = out[at, :] + added[f, pl.ds(first, sizes.half), :]
    for half, edge in ((own_half, own_edge), (sibling_half, sibling_edge)):

        def load(f, row, count):
            return half[pl.ds(sizes.half_at(f) + row, count), :]

        @pl.when(core == 0)
        def _():
            south_edge(sizes, load, edge)

        @pl.when(core == 1)
        def _():
            north_edge(sizes, load, edge, sizes.half)


ORIGIN = 16


def put_south(sizes, buf, edge):
    for f in range(4):
        put(buf, f, ORIGIN - sizes.body, sizes.body, edge, sizes.edge_at(f))
        put(buf, f, ORIGIN - REACH, sizes.tail, edge, sizes.tail_at(f))


def put_north(sizes, buf, edge):
    for f in range(4):
        put(buf, f, ORIGIN + sizes.rows, sizes.body, edge, sizes.edge_at(f))
        put(buf, f, ORIGIN + sizes.rows + sizes.body, sizes.tail, edge, sizes.tail_at(f))


def before_kernel(sizes, domains, state, edge_one, edge_two, mine, other, score, *bufs):
    rows, half = sizes.rows, sizes.half
    total_rows = rows * domains
    domain = lax.axis_index("domain")
    parity = lax.rem(domain, 2)
    core = lax.rem(lax.axis_index("member"), 2)
    start = bufs[0]
    chunks = start.shape[1]
    for f in range(4):
        put(start, f, ORIGIN, rows, state.at[f], 0)

    @pl.when(parity == 0)
    def _():
        put_north(sizes, start, edge_one)
        put_south(sizes, start, edge_two)

    @pl.when(parity == 1)
    def _():
        put_south(sizes, start, edge_one)
        put_north(sizes, start, edge_two)

    advance(bufs, ORIGIN, rows, REACH, domain, domains, total_rows)
    for f in range(4):
        for j in range(chunks):
            at = (pl.ds(sizes.half_at(f), half), pl.ds(j * LANES, LANES))
            first = pl.multiple_of(ORIGIN + core * half, SUB)
            mine[at] = start[f, j, pl.ds(first, half), :]
            first = pl.multiple_of(ORIGIN + (1 - core) * half, SUB)
            other[at] = start[f, j, pl.ds(first, half), :]
    sub = lax.broadcasted_iota(jnp.int32, (SUB, LANES), 0)
    total = jnp.zeros((SUB, LANES), jnp.float32)
    for row in range(0, rows, SUB):
        line = jnp.zeros((SUB, LANES), jnp.float32)
        for j in range(chunks):
            q = start[3, j, pl.ds(ORIGIN + row, SUB), :]
            line = line + q * q
        place = (sub + (row + domain * rows)).astype(jnp.float32)
        total = total + (1.0 + 2.0 * place / (total_rows - 1)) * line
    score[...] = total


def after_kernel(
    sizes, domains, own_half, far_half, near_halo, far_halo, score_one, score_two, out, score, *bufs
):
    rows, half = sizes.rows, sizes.half
    total_rows = rows * domains
    domain = lax.axis_index("domain")
    core = lax.rem(lax.axis_index("member"), 2)
    start = bufs[0]
    chunks = start.shape[1]
    score[0, 0] = jnp.sum(score_one[...] + score_two[...]) / (total_rows * out.shape[2])
    for f in range(4):
        at = sizes.half_at(f)
        put(start, f, pl.multiple_of(ORIGIN + core * half, SUB), half, own_half, at)
        put(start, f, pl.multiple_of(ORIGIN + (1 - core) * half, SUB), half, far_half, at)

    @pl.when(core == 0)
    def _():
        put_south(sizes, start, near_halo)
        put_north(sizes, start, far_halo)

    @pl.when(core == 1)
    def _():
        put_south(sizes, start, far_halo)
        put_north(sizes, start, near_halo)

    advance(bufs, ORIGIN, rows, REACH, domain, domains, total_rows)
    for f in range(4):
        for j in range(chunks):
            out[f, :, pl.ds(j * LANES, LANES)] = start[f, j, pl.ds(ORIGIN, rows), :]


def chip_grid(chips):
    b = 1
    while chips % (2 * b) == 0 and (2 * b) * (2 * b) <= chips:
        b *= 2
    return chips // b, b


def on_device(state, perturbation, parents, members, domains):
    state, perturbation = state[0], perturbation[0]
    rows, width = state.shape[1:]
    sizes = Sizes(rows)
    chunks = width // LANES
    chips = chip_grid(members // 2)
    chips_a, chips_b = chips
    hops = max(chips)
    params = pltpu.CompilerParams(vmem_limit_bytes=40 * 2**20)
    half_shape = jax.ShapeDtypeStruct((sizes.half_rows, width), jnp.float32)
    score_shape = jax.ShapeDtypeStruct((SUB, LANES), jnp.float32)
    edge_shape = jax.ShapeDtypeStruct((sizes.edge_rows, width), jnp.float32)

    def member(a, b, core):
        return ((a % chips_a) * chips_b + b % chips_b) * 2 + core

    everywhere = [(a, b) for a in range(chips_a) for b in range(chips_b)]
    sibling = [(i, i ^ 1) for i in range(members)]

    def same_core(first, k):
        pairs = []
        for a, b in everywhere:
            if k < (chips_b if first else chips_a):
                pairs.append((member(a, b, 0), member(a, b + k, 0) if first else member(a + k, b, 0)))
            if k < (chips_a if first else chips_b):
                pairs.append((member(a, b, 1), member(a + k, b, 1) if first else member(a, b + k, 1)))
        return pairs

    def other_core(k):
        pairs = []
        for a, b in everywhere:
            if k < chips_a:
                pairs.append((member(a, b, 0), member(a + k, b, 1)))
            if k < chips_b:
                pairs.append((member(a, b, 1), member(a, b + k, 0)))
        return pairs

    def flat(m, z):
        return m * domains + z

    levels = range(domains)
    near = members // 2 % 2 == 0

    def matched(partner):
        return [
            (flat(m, z), flat(m, partner(z)) if 0 <= partner(z) < domains else flat(m ^ 1, z))
            for m in range(members)
            for z in levels
        ]

    pair_one = matched(lambda z: z ^ 1)
    pair_two = matched(lambda z: ((z + 1) ^ 1) - 1)
    to_other, to_same = [], []
    for m in range(members):
        core = m % 2
        for z in levels:
            level = z + 1 if core else z - 1
            if 0 <= level < domains:
                to_other.append((flat(m, z), flat(m ^ 1, level)))
                to_same.append((flat(m, z), flat(m, level)))
            else:
                if near:
                    to_other.append((flat(m, z), flat(m ^ 2, z)))
                to_same.append((flat(m, z), flat(m ^ 1, z)))
    both = ("member", "domain")

    def call(kernel, out_shape, in_specs, out_specs, scratch=()):
        return pl.pallas_call(
            kernel,
            out_shape=out_shape,
            in_specs=in_specs,
            out_specs=out_specs,
            scratch_shapes=scratch,
            compiler_params=params,
        )

    bufs = [pltpu.VMEM((4, chunks, rows + 32, LANES), jnp.float32)] * 3
    edge_one, edge_two = call(
        functools.partial(edges_kernel, sizes), (edge_shape,) * 2, [VMEM], (VMEM,) * 2
    )(state)
    edge_one = lax.ppermute(edge_one, both, pair_one)
    edge_two = lax.ppermute(edge_two, both, pair_two)
    sibling_pert = lax.ppermute(perturbation, "member", sibling)
    routes = call(
        functools.partial(routes_kernel, chips, hops),
        jax.ShapeDtypeStruct(((2 * hops + 2) * SUB, LANES), jnp.int32),
        [SMEM],
        VMEM,
    )(parents)

    mine, other, score = call(
        functools.partial(before_kernel, sizes, domains),
        (half_shape, half_shape, score_shape),
        [VMEM] * 3,
        (VMEM,) * 3,
        bufs,
    )(state, edge_one, edge_two)

    held = [mine, lax.ppermute(other, "member", sibling)]
    for k in range(1, hops):
        held.append(lax.ppermute(mine, "member", same_core(True, k)))
        held.append(lax.ppermute(other, "member", other_core(k)))

    scores = [score, jnp.zeros_like(score)]
    if domains & (domains - 1) == 0:
        bit = 1
        while bit < domains:
            score = scores[0] if bit == 1 else scores[0] + scores[1]
            pairs = [(z, z ^ bit) for z in range(domains)]
            scores = [score, lax.ppermute(score, "domain", pairs)]
            bit *= 2
    else:
        scores[0] = lax.psum(score, "domain")

    picked = call(
        functools.partial(pick_kernel, hops),
        (half_shape,) * (2 * hops),
        [VMEM] * (2 * hops + 2),
        (VMEM,) * (2 * hops),
    )(routes, *held, scores[0])

    own, other = [picked[0]], [picked[1]]
    for k in range(1, hops):
        own.append(lax.ppermute(picked[2 * k], "member", same_core(False, k)))
        other.append(lax.ppermute(picked[2 * k + 1], "member", same_core(False, k)))
    own_half, sibling_half, own_edge, sibling_edge = call(
        functools.partial(settle_kernel, sizes, hops),
        (half_shape, half_shape, edge_shape, edge_shape),
        [VMEM] * (2 * hops + 4),
        (VMEM,) * 4,
    )(routes, perturbation, sibling_pert, *own, *other, scores[1])
    near_halo = lax.ppermute(sibling_edge, both, to_other)
    far_halo = lax.ppermute(own_edge, both, to_same)
    far_half = lax.ppermute(sibling_half, "member", sibling)

    after, score = call(
        functools.partial(after_kernel, sizes, domains),
        (
            jax.ShapeDtypeStruct((4, rows, width), jnp.float32),
            jax.ShapeDtypeStruct((1, 1), jnp.float32),
        ),
        [VMEM] * 6,
        (VMEM, SMEM),
        bufs,
    )(own_half, far_half, near_halo, far_halo, *scores)
    return after[None], jnp.reshape(score, (1,))


def solution(mesh):
    placed = (P("member", None, "domain", None), P("member", None, "domain", None), P())
    return jax.shard_map(
        functools.partial(
            on_device, members=mesh.shape["member"], domains=mesh.shape["domain"]
        ),
        mesh=mesh,
        in_specs=placed,
        out_specs=(P("member", None, "domain", None), P("member")),
        check_vma=False,
    )
```

```python
import functools

import jax
import jax.numpy as jnp
from jax import lax
from jax.experimental import pallas as pl
from jax.experimental.pallas import tpu as pltpu
from jax.sharding import PartitionSpec as P

STEPS = 3
REACH = 3 * STEPS

time_step = 0.1
viscous = 0.05
coriolis = 1.0

LANES = 128
SUB = 8
VMEM = pl.BlockSpec(memory_space=pltpu.VMEM)
SMEM = pl.BlockSpec(memory_space=pltpu.SMEM)


def stage(src, base, dst, first, count, keep, gain, scales, turn, walls, fields):
    scale, scale_out = scales
    chunks = src.shape[1]
    lane = lax.broadcasted_iota(jnp.int32, (SUB, LANES), 1)
    sub = lax.broadcasted_iota(jnp.int32, (SUB, LANES), 0)
    at_last = lane == LANES - 1
    at_first = lane == 0
    step = gain * time_step
    linear = scale_out / scale
    quadratic = -0.5 * step * linear / scale
    diffuse = step * viscous * linear
    middle = (gain - 4.0 * step * viscous) * linear
    slope = 0.5 * step * linear
    keep = keep * scale_out
    turn_first, turn_slope = turn
    for row in range(first, first + count, SUB):

        def load(field, chunk, offset):
            return src[field, chunk, pl.ds(row + offset, SUB), :]

        cells = [[load(f, j, 0) for j in range(chunks)] for f in range(4)]
        to_west = [[pltpu.roll(c, LANES - 1, 1) for c in line] for line in cells]
        to_east = [[pltpu.roll(c, 1, 1) for c in line] for line in cells]
        spin = (turn_first + row * turn_slope) * (step * linear)
        outside = [(sub == at - row) & flag for at, flag in walls if row <= at < row + SUB]
        for j in range(chunks):
            c = [cells[f][j] for f in range(4)]
            n = [load(f, j, 1) for f in range(4)]
            s = [load(f, j, -1) for f in range(4)]
            e = [jnp.where(at_last, to_west[f][(j + 1) % chunks], to_west[f][j]) for f in range(4)]
            w = [jnp.where(at_first, to_east[f][(j - 1) % chunks], to_east[f][j]) for f in range(4)]
            u = c[1] * quadratic
            v = c[2] * quadratic
            by_e, by_w, by_n, by_s = diffuse + u, diffuse - u, diffuse + v, diffuse - v
            for f in fields:
                if f == 0:
                    near = (e[0] + w[0]) + (n[0] + s[0])
                    flux = ((scale + e[0]) * e[1] - (scale + w[0]) * w[1]) + (
                        (scale + n[0]) * n[2] - (scale + s[0]) * s[2]
                    )
                    out = near * diffuse + flux * quadratic
                else:
                    out = (e[f] * by_e + w[f] * by_w) + (n[f] * by_n + s[f] * by_s)
                if f == 1:
                    out = out + (spin * c[2] - (e[0] - w[0]) * slope)
                if f == 2:
                    out = out - (spin * c[1] + (n[0] - s[0]) * slope)
                out = out + (c[f] if abs(middle - 1.0) < 1e-12 else c[f] * middle)
                if keep:
                    kept = base[f, j, pl.ds(row, SUB), :]
                    out = out + (kept if abs(keep - 1.0) < 1e-12 else kept * keep)
                for hide in outside:
                    out = jnp.where(hide, 0.0, out)
                dst[f, j, pl.ds(row, SUB), :] = out


def advance(bufs, origin, rows, reach, domain, domains, total_rows, last_fields=(0, 1, 2, 3)):
    state, one, two = bufs
    sub = lax.broadcasted_iota(jnp.int32, (SUB, LANES), 0)
    slope = 2.0 * coriolis / total_rows
    turn_first = ((sub + (domain * rows - origin)).astype(jnp.float32) + 0.5) * slope - coriolis
    walls = [
        (origin - 1, jnp.full((SUB, LANES), domain, jnp.int32) == 0),
        (origin + rows, jnp.full((SUB, LANES), domain, jnp.int32) == domains - 1),
    ]
    for at, flag in walls:
        for f in range(4):
            for j in range(state.shape[1]):
                line = state[f, j, pl.ds(at, 1), :]
                state[f, j, pl.ds(at, 1), :] = jnp.where(flag[:1], 0.0, line)
    scale_one = 1.0 / (1.0 - 4.0 * time_step * viscous)
    scale_two = 1.0 / 0.75
    thirds = (
        (state, one, 0.0, 1.0, (1.0, scale_one)),
        (one, two, 0.75, 0.25, (scale_one, scale_two)),
        (two, state, 1.0 / 3.0, 2.0 / 3.0, (scale_two, 1.0)),
    )
    for number in range(3 * STEPS):
        src, dst, keep, gain, scales = thirds[number % 3]
        reach -= 1
        first, count = origin - reach, rows + 2 * reach
        fields = range(4) if number < 3 * STEPS - 1 else last_fields
        stage(src, state, dst, first, count, keep, gain, scales, (turn_first, slope), walls, fields)


def put(buf, field, row, count, block, row_from, add=False):
    for j in range(buf.shape[1]):
        piece = block[pl.ds(row_from, count), pl.ds(j * LANES, LANES)]
        if add:
            piece = piece + buf[field, j, pl.ds(row, count), :]
        buf[field, j, pl.ds(row, count), :] = piece


class Sizes:
    def __init__(self, rows):
        self.rows = rows
        self.half = rows // 2
        self.extra = max(0, 2 * REACH - self.half)
        self.half_rows = 4 * (self.half + self.extra)
        self.body = REACH // SUB * SUB
        self.tail = REACH - self.body
        self.edge_rows = 8 * REACH

    def half_at(self, field):
        return field * self.half

    def extra_at(self, field):
        return 4 * self.half + field * self.extra

    def edge_at(self, which, field):
        return (which * 4 + field) * self.body

    def tail_at(self, which, field):
        return 8 * self.body + (which * 4 + field) * self.tail


def pack_kernel(sizes, state, mine, other):
    rows, half, extra = sizes.rows, sizes.half, sizes.extra
    core = lax.rem(lax.axis_index("member"), 2)

    def south_half(out):
        for f in range(4):
            out[pl.ds(sizes.half_at(f), half), :] = state[f, pl.ds(0, half), :]
            out[pl.ds(sizes.extra_at(f), extra), :] = state[f, pl.ds(half, extra), :]

    def north_half(out):
        for f in range(4):
            out[pl.ds(sizes.half_at(f), half), :] = state[f, pl.ds(rows - half, half), :]
            out[pl.ds(sizes.extra_at(f), extra), :] = state[f, pl.ds(rows - half - extra, extra), :]

    @pl.when(core == 0)
    def _():
        south_half(mine)
        north_half(other)

    @pl.when(core == 1)
    def _():
        north_half(mine)
        south_half(other)


def edges_kernel(sizes, state, pert, _, edge_one, edge_two):
    rows, body, tail = sizes.rows, sizes.body, sizes.tail
    parity = lax.rem(lax.axis_index("domain"), 2)

    def south_edge(out):
        for k, a in enumerate((state, pert)):
            for f in range(4):
                out[pl.ds(sizes.edge_at(k, f), body), :] = a[f, pl.ds(0, body), :]
                out[pl.ds(sizes.tail_at(k, f), tail), :] = a[f, pl.ds(body, tail), :]

    def north_edge(out):
        for k, a in enumerate((state, pert)):
            for f in range(4):
                out[pl.ds(sizes.edge_at(k, f), body), :] = a[f, pl.ds(rows - body, body), :]
                out[pl.ds(sizes.tail_at(k, f), tail), :] = a[f, pl.ds(rows - REACH, tail), :]

    @pl.when(parity == 0)
    def _():
        north_edge(edge_one)
        south_edge(edge_two)

    @pl.when(parity == 1)
    def _():
        south_edge(edge_one)
        north_edge(edge_two)


class Place:
    def __init__(self, chips_a, chips_b):
        self.sizes = (chips_a, chips_b)
        member = lax.axis_index("member")
        self.core = lax.rem(member, 2)
        chip = member // 2
        self.a, self.b = chip // chips_b, lax.rem(chip, chips_b)

    def child(self, hop, core):
        chips_a, chips_b = self.sizes
        a = jnp.where(self.core == 0, lax.rem(self.a + hop, chips_a), self.a)
        b = jnp.where(self.core == 0, self.b, lax.rem(self.b + hop, chips_b))
        return (a * chips_b + b) * 2 + core

    def first_hop(self, parent):
        chips_a, chips_b = self.sizes
        chip = parent // 2
        a, b = chip // chips_b, lax.rem(chip, chips_b)
        return jnp.where(
            self.core == 0,
            lax.rem(self.b - b + chips_b, chips_b),
            lax.rem(self.a - a + chips_a, chips_a),
        )

    def second_hop(self, parent):
        chips_a, chips_b = self.sizes
        chip = parent // 2
        a, b = chip // chips_b, lax.rem(chip, chips_b)
        return jnp.where(
            self.core == 0,
            lax.rem(self.a - a + chips_a, chips_a),
            lax.rem(self.b - b + chips_b, chips_b),
        )


def parent_of(parents, member):
    return jnp.clip(parents[member], 0, parents.shape[0] - 1)


def routes_kernel(chips, hops, parents, out):
    place = Place(*chips)
    tile = 0
    for hop in range(hops):
        for own in (True, False):
            core = place.core if own else 1 - place.core
            parent = parent_of(parents, place.child(hop, core))
            same = jnp.where(lax.rem(parent, 2) == place.core, 0, 1)
            index = 2 * place.first_hop(parent) + same
            out[pl.ds(tile * SUB, SUB), :] = jnp.full((SUB, LANES), index, jnp.int32)
            tile += 1
    for own in (True, False):
        core = place.core if own else 1 - place.core
        index = place.second_hop(parent_of(parents, place.child(0, core)))
        out[pl.ds(tile * SUB, SUB), :] = jnp.full((SUB, LANES), index, jnp.int32)
        tile += 1


def choose(routes, tile, sources, out):
    index = routes[pl.ds(tile * SUB, SUB), :]
    takes = [index == k for k in range(1, len(sources))]
    for row in range(0, out.shape[0], SUB):
        for lane in range(0, out.shape[1], LANES):
            where = (pl.ds(row, SUB), pl.ds(lane, LANES))
            value = sources[0][where]
            for take, source in zip(takes, sources[1:]):
                value = jnp.where(take, source[where], value)
            out[where] = value


def pick_kernel(hops, routes, *refs):
    held, outs = refs[: 2 * hops], refs[-2 * hops :]
    for tile, out in enumerate(outs):
        choose(routes, tile, held, out)


def settle_kernel(hops, routes, *refs):
    own_half, sibling_half = refs[-2:]
    choose(routes, 2 * hops, refs[:hops], own_half)
    choose(routes, 2 * hops + 1, refs[hops : 2 * hops], sibling_half)


def put_edges(sizes, which, buf, origin, edge_one, edge_two, add=False):
    rows, body, tail = sizes.rows, sizes.body, sizes.tail
    parity = lax.rem(lax.axis_index("domain"), 2)

    def south(edge):
        for f in range(4):
            put(buf, f, origin - body, body, edge, sizes.edge_at(which, f), add)
            put(buf, f, origin - REACH, tail, edge, sizes.tail_at(which, f), add)

    def north(edge):
        for f in range(4):
            put(buf, f, origin + rows, body, edge, sizes.edge_at(which, f), add)
            put(buf, f, origin + rows + body, tail, edge, sizes.tail_at(which, f), add)

    @pl.when(parity == 0)
    def _():
        north(edge_one)
        south(edge_two)

    @pl.when(parity == 1)
    def _():
        south(edge_one)
        north(edge_two)


def score_kernel(sizes, domains, state, edge_one, edge_two, _, out, *bufs):
    rows = sizes.rows
    origin = 16
    total_rows = rows * domains
    domain = lax.axis_index("domain")
    for f in range(4):
        put(bufs[0], f, origin, rows, state.at[f], 0)
    put_edges(sizes, 0, bufs[0], origin, edge_one, edge_two)
    advance(bufs, origin, rows, REACH, domain, domains, total_rows, (3,))
    sub = lax.broadcasted_iota(jnp.int32, (SUB, LANES), 0)
    total = jnp.zeros((SUB, LANES), jnp.float32)
    for row in range(0, rows, SUB):
        line = jnp.zeros((SUB, LANES), jnp.float32)
        for j in range(bufs[0].shape[1]):
            q = bufs[0][3, j, pl.ds(origin + row, SUB), :]
            line = line + q * q
        place = (sub + (row + domain * rows)).astype(jnp.float32)
        total = total + (1.0 + 2.0 * place / (total_rows - 1)) * line
    out[...] = total


def total_kernel(cells, score_one, score_two, _, out):
    out[0, 0] = jnp.sum(score_one[...] + score_two[...]) / cells


def final_kernel(
    sizes, domains, own_half, far_half, near_halo, far_halo, pert, edge_one, edge_two, out, last, *bufs
):
    last[...] = jnp.zeros((SUB, LANES), jnp.float32)
    rows, half, extra = sizes.rows, sizes.half, sizes.extra
    origin = 24
    total_rows = rows * domains
    domain = lax.axis_index("domain")
    core = lax.rem(lax.axis_index("member"), 2)
    start = bufs[0]

    def fill(south, north, south_halo, north_halo):
        for f in range(4):
            at, more = sizes.half_at(f), sizes.extra_at(f)
            put(start, f, origin - half, half, south_halo, at)
            put(start, f, origin - half - extra, extra, south_halo, more)
            put(start, f, origin, half, south, at)
            put(start, f, origin + half, half, north, at)
            put(start, f, origin + rows, half, north_halo, at)
            put(start, f, origin + rows + half, extra, north_halo, more)

    @pl.when(core == 0)
    def _():
        fill(own_half, far_half, near_halo, far_halo)

    @pl.when(core == 1)
    def _():
        fill(far_half, own_half, far_halo, near_halo)

    advance(bufs, origin, rows, 2 * REACH, domain, domains, total_rows)
    for f in range(4):
        put(start, f, origin, rows, pert.at[f], 0, add=True)
    put_edges(sizes, 1, start, origin, edge_one, edge_two, add=True)
    advance(bufs, origin, rows, REACH, domain, domains, total_rows)
    for f in range(4):
        for j in range(start.shape[1]):
            out[f, :, pl.ds(j * LANES, LANES)] = start[f, j, pl.ds(origin, rows), :]


def chip_grid(chips):
    b = 1
    while chips % (2 * b) == 0 and (2 * b) * (2 * b) <= chips:
        b *= 2
    return chips // b, b


def on_device(state, perturbation, parents, members, domains):
    state, perturbation = state[0], perturbation[0]
    rows, width = state.shape[1:]
    sizes = Sizes(rows)
    chunks = width // LANES
    chips = chip_grid(members // 2)
    chips_a, chips_b = chips
    hops = max(chips)
    params = pltpu.CompilerParams(vmem_limit_bytes=40 * 2**20)
    half_shape = jax.ShapeDtypeStruct((sizes.half_rows, width), jnp.float32)
    score_shape = jax.ShapeDtypeStruct((SUB, LANES), jnp.float32)
    edge_shape = jax.ShapeDtypeStruct((sizes.edge_rows, width), jnp.float32)

    def member(a, b, core):
        return ((a % chips_a) * chips_b + b % chips_b) * 2 + core

    everywhere = [(a, b) for a in range(chips_a) for b in range(chips_b)]
    sibling = [(i, i ^ 1) for i in range(members)]

    def same_core(first, k):
        pairs = []
        for a, b in everywhere:
            if k < (chips_b if first else chips_a):
                pairs.append((member(a, b, 0), member(a, b + k, 0) if first else member(a + k, b, 0)))
            if k < (chips_a if first else chips_b):
                pairs.append((member(a, b, 1), member(a + k, b, 1) if first else member(a, b + k, 1)))
        return pairs

    def other_core(k):
        pairs = []
        for a, b in everywhere:
            if k < chips_a:
                pairs.append((member(a, b, 0), member(a + k, b, 1)))
            if k < chips_b:
                pairs.append((member(a, b, 1), member(a, b + k, 0)))
        return pairs

    def flat(m, z):
        return m * domains + z

    levels = range(domains)
    near = members // 2 % 2 == 0

    def matched(partner):
        return [
            (flat(m, z), flat(m, partner(z)) if 0 <= partner(z) < domains else flat(m ^ 1, z))
            for m in range(members)
            for z in levels
        ]

    pair_one = matched(lambda z: z ^ 1)
    pair_two = matched(lambda z: ((z + 1) ^ 1) - 1)
    to_other, to_same = [], []
    for m in range(members):
        core = m % 2
        for z in levels:
            level = z + 1 if core else z - 1
            if 0 <= level < domains:
                to_other.append((flat(m, z), flat(m ^ 1, level)))
                to_same.append((flat(m, z), flat(m, level)))
            else:
                if near:
                    to_other.append((flat(m, z), flat(m ^ 2, z)))
                to_same.append((flat(m, z), flat(m ^ 1, z)))
    both = ("member", "domain")

    def call(kernel, out_shape, in_specs, out_specs, scratch=()):
        return pl.pallas_call(
            kernel,
            out_shape=out_shape,
            in_specs=in_specs,
            out_specs=out_specs,
            scratch_shapes=scratch,
            compiler_params=params,
        )

    mine, other = call(
        functools.partial(pack_kernel, sizes), (half_shape,) * 2, [VMEM], (VMEM,) * 2
    )(state)
    held = [mine, lax.ppermute(other, "member", sibling)]
    for k in range(1, hops):
        held.append(lax.ppermute(mine, "member", same_core(True, k)))
        held.append(lax.ppermute(other, "member", other_core(k)))
    edge_one, edge_two = call(
        functools.partial(edges_kernel, sizes), (edge_shape,) * 2, [VMEM] * 3, (VMEM,) * 2
    )(state, perturbation, held[1])
    edge_one = lax.ppermute(edge_one, both, pair_one)
    edge_two = lax.ppermute(edge_two, both, pair_two)
    routes = call(
        functools.partial(routes_kernel, chips, hops),
        jax.ShapeDtypeStruct(((2 * hops + 2) * SUB, LANES), jnp.int32),
        [SMEM],
        VMEM,
    )(parents)

    picked = call(
        functools.partial(pick_kernel, hops),
        (half_shape,) * (2 * hops),
        [VMEM] * (2 * hops + 1),
        (VMEM,) * (2 * hops),
    )(routes, *held)

    score = call(
        functools.partial(score_kernel, sizes, domains),
        score_shape,
        [VMEM] * 4,
        VMEM,
        [pltpu.VMEM((4, chunks, rows + 32, LANES), jnp.float32)] * 3,
    )(state, edge_one, edge_two, picked[0])
    scores = [score, jnp.zeros_like(score)]
    bit = 1
    if domains & (domains - 1):
        scores[0] = lax.psum(score, "domain")
    while bit < domains and domains & (domains - 1) == 0:
        score = scores[0] if bit == 1 else scores[0] + scores[1]
        pairs = [(z, z ^ bit) for z in range(domains)]
        scores = [score, lax.ppermute(score, "domain", pairs)]
        bit *= 2

    own, other = [picked[0]], [picked[1]]
    for k in range(1, hops):
        own.append(lax.ppermute(picked[2 * k], "member", same_core(False, k)))
        other.append(lax.ppermute(picked[2 * k + 1], "member", same_core(False, k)))
    own_half, sibling_half = call(
        functools.partial(settle_kernel, hops),
        (half_shape, half_shape),
        [VMEM] * (2 * hops + 2),
        (VMEM,) * 2,
    )(routes, *own, *other, score)
    near_halo = lax.ppermute(sibling_half, both, to_other)
    far_halo = lax.ppermute(own_half, both, to_same)
    far_half = lax.ppermute(sibling_half, "member", sibling)
    after, last = call(
        functools.partial(final_kernel, sizes, domains),
        (jax.ShapeDtypeStruct((4, rows, width), jnp.float32), score_shape),
        [VMEM] * 7,
        (VMEM,) * 2,
        [pltpu.VMEM((4, chunks, rows + 48, LANES), jnp.float32)] * 3,
    )(own_half, far_half, near_halo, far_halo, perturbation, edge_one, edge_two)
    score = call(
        functools.partial(total_kernel, rows * domains * width),
        jax.ShapeDtypeStruct((1, 1), jnp.float32),
        [VMEM] * 3,
        SMEM,
    )(*scores, last)
    return after[None], jnp.reshape(score, (1,))


def solution(mesh):
    placed = (P("member", None, "domain", None), P("member", None, "domain", None), P())
    return jax.shard_map(
        functools.partial(
            on_device, members=mesh.shape["member"], domains=mesh.shape["domain"]
        ),
        mesh=mesh,
        in_specs=placed,
        out_specs=(P("member", None, "domain", None), P("member")),
        check_vma=False,
    )
```

```python
import functools

import jax
import jax.numpy as jnp
from jax import lax
from jax.experimental import pallas as pl
from jax.experimental.pallas import tpu as pltpu
from jax.sharding import PartitionSpec as P

STEPS = 3
REACH = 3 * STEPS
WIDE = 16

time_step = 0.1
viscous = 0.05
coriolis = 1.0

LANES = 128
SUB = 8
VMEM = pl.BlockSpec(memory_space=pltpu.VMEM)
SMEM = pl.BlockSpec(memory_space=pltpu.SMEM)


def stage(src, base, dst, first, count, keep, gain, scales, turn, walls, fields):
    scale, scale_out = scales
    chunks = src.shape[1]
    lane = lax.broadcasted_iota(jnp.int32, (SUB, LANES), 1)
    sub = lax.broadcasted_iota(jnp.int32, (SUB, LANES), 0)
    at_last = lane == LANES - 1
    at_first = lane == 0
    step = gain * time_step
    linear = scale_out / scale
    quadratic = -0.5 * step * linear / scale
    diffuse = step * viscous * linear
    middle = (gain - 4.0 * step * viscous) * linear
    slope = 0.5 * step * linear
    keep = keep * scale_out
    turn_first, turn_slope = turn
    for row in range(first, first + count, SUB):

        def load(field, chunk, offset):
            return src[field, chunk, pl.ds(row + offset, SUB), :]

        cells = [[load(f, j, 0) for j in range(chunks)] for f in range(4)]
        to_west = [[pltpu.roll(c, LANES - 1, 1) for c in line] for line in cells]
        to_east = [[pltpu.roll(c, 1, 1) for c in line] for line in cells]
        spin = (turn_first + row * turn_slope) * (step * linear)
        outside = [(sub == at - row) & flag for at, flag in walls if row <= at < row + SUB]
        for j in range(chunks):
            c = [cells[f][j] for f in range(4)]
            n = [load(f, j, 1) for f in range(4)]
            s = [load(f, j, -1) for f in range(4)]
            e = [jnp.where(at_last, to_west[f][(j + 1) % chunks], to_west[f][j]) for f in range(4)]
            w = [jnp.where(at_first, to_east[f][(j - 1) % chunks], to_east[f][j]) for f in range(4)]
            u = c[1] * quadratic
            v = c[2] * quadratic
            by_e, by_w, by_n, by_s = diffuse + u, diffuse - u, diffuse + v, diffuse - v
            for f in fields:
                if f == 0:
                    near = (e[0] + w[0]) + (n[0] + s[0])
                    flux = ((scale + e[0]) * e[1] - (scale + w[0]) * w[1]) + (
                        (scale + n[0]) * n[2] - (scale + s[0]) * s[2]
                    )
                    out = near * diffuse + flux * quadratic
                else:
                    out = (e[f] * by_e + w[f] * by_w) + (n[f] * by_n + s[f] * by_s)
                if f == 1:
                    out = out + (spin * c[2] - (e[0] - w[0]) * slope)
                if f == 2:
                    out = out - (spin * c[1] + (n[0] - s[0]) * slope)
                out = out + (c[f] if abs(middle - 1.0) < 1e-12 else c[f] * middle)
                if keep:
                    kept = base[f, j, pl.ds(row, SUB), :]
                    out = out + (kept if abs(keep - 1.0) < 1e-12 else kept * keep)
                for hide in outside:
                    out = jnp.where(hide, 0.0, out)
                dst[f, j, pl.ds(row, SUB), :] = out


def advance(bufs, origin, rows, reach, domain, domains, total_rows, last_fields=(0, 1, 2, 3)):
    state, one, two = bufs
    sub = lax.broadcasted_iota(jnp.int32, (SUB, LANES), 0)
    slope = 2.0 * coriolis / total_rows
    turn_first = ((sub + (domain * rows - origin)).astype(jnp.float32) + 0.5) * slope - coriolis
    walls = [
        (origin - 1, jnp.full((SUB, LANES), domain, jnp.int32) == 0),
        (origin + rows, jnp.full((SUB, LANES), domain, jnp.int32) == domains - 1),
    ]
    for at, flag in walls:
        for f in range(4):
            for j in range(state.shape[1]):
                line = state[f, j, pl.ds(at, 1), :]
                state[f, j, pl.ds(at, 1), :] = jnp.where(flag[:1], 0.0, line)
    scale_one = 1.0 / (1.0 - 4.0 * time_step * viscous)
    scale_two = 1.0 / 0.75
    thirds = (
        (state, one, 0.0, 1.0, (1.0, scale_one)),
        (one, two, 0.75, 0.25, (scale_one, scale_two)),
        (two, state, 1.0 / 3.0, 2.0 / 3.0, (scale_two, 1.0)),
    )
    for number in range(3 * STEPS):
        src, dst, keep, gain, scales = thirds[number % 3]
        reach -= 1
        first, count = origin - reach, rows + 2 * reach
        fields = range(4) if number < 3 * STEPS - 1 else last_fields
        stage(src, state, dst, first, count, keep, gain, scales, (turn_first, slope), walls, fields)


def put(buf, field, row, count, block, row_from, add=False):
    for j in range(buf.shape[1]):
        piece = block[pl.ds(row_from, count), pl.ds(j * LANES, LANES)]
        if add:
            piece = piece + buf[field, j, pl.ds(row, count), :]
        buf[field, j, pl.ds(row, count), :] = piece


class Sizes:
    def __init__(self, rows):
        self.rows = rows
        self.half = rows // 2
        self.extra = max(0, 2 * REACH - self.half)
        self.half_rows = 4 * (self.half + self.extra)
        self.body = REACH // SUB * SUB
        self.tail = REACH - self.body
        self.edge_rows = 8 * REACH

    def half_at(self, field):
        return field * self.half

    def extra_at(self, field):
        return 4 * self.half + field * self.extra

    def edge_at(self, which, field):
        return (which * 4 + field) * self.body

    def tail_at(self, which, field):
        return 8 * self.body + (which * 4 + field) * self.tail


def pack_kernel(sizes, state, mine, other):
    rows, half, extra = sizes.rows, sizes.half, sizes.extra
    core = lax.rem(lax.axis_index("member"), 2)

    def south_half(out):
        for f in range(4):
            out[pl.ds(sizes.half_at(f), half), :] = state[f, pl.ds(0, half), :]
            out[pl.ds(sizes.extra_at(f), extra), :] = state[f, pl.ds(half, extra), :]

    def north_half(out):
        for f in range(4):
            out[pl.ds(sizes.half_at(f), half), :] = state[f, pl.ds(rows - half, half), :]
            out[pl.ds(sizes.extra_at(f), extra), :] = state[f, pl.ds(rows - half - extra, extra), :]

    @pl.when(core == 0)
    def _():
        south_half(mine)
        north_half(other)

    @pl.when(core == 1)
    def _():
        north_half(mine)
        south_half(other)


def edges_kernel(sizes, state, pert, _, edge_one, edge_two):
    rows, body, tail = sizes.rows, sizes.body, sizes.tail
    parity = lax.rem(lax.axis_index("domain"), 2)

    def south_edge(out):
        for k, a in enumerate((state, pert)):
            for f in range(4):
                out[pl.ds(sizes.edge_at(k, f), body), :] = a[f, pl.ds(0, body), :]
                out[pl.ds(sizes.tail_at(k, f), tail), :] = a[f, pl.ds(body, tail), :]

    def north_edge(out):
        for k, a in enumerate((state, pert)):
            for f in range(4):
                out[pl.ds(sizes.edge_at(k, f), body), :] = a[f, pl.ds(rows - body, body), :]
                out[pl.ds(sizes.tail_at(k, f), tail), :] = a[f, pl.ds(rows - REACH, tail), :]

    @pl.when(parity == 0)
    def _():
        north_edge(edge_one)
        south_edge(edge_two)

    @pl.when(parity == 1)
    def _():
        south_edge(edge_one)
        north_edge(edge_two)


class Place:
    def __init__(self, chips_a, chips_b):
        self.sizes = (chips_a, chips_b)
        member = lax.axis_index("member")
        self.core = lax.rem(member, 2)
        chip = member // 2
        self.a, self.b = chip // chips_b, lax.rem(chip, chips_b)

    def child(self, hop, core):
        chips_a, chips_b = self.sizes
        a = jnp.where(self.core == 0, lax.rem(self.a + hop, chips_a), self.a)
        b = jnp.where(self.core == 0, self.b, lax.rem(self.b + hop, chips_b))
        return (a * chips_b + b) * 2 + core

    def first_hop(self, parent):
        chips_a, chips_b = self.sizes
        chip = parent // 2
        a, b = chip // chips_b, lax.rem(chip, chips_b)
        return jnp.where(
            self.core == 0,
            lax.rem(self.b - b + chips_b, chips_b),
            lax.rem(self.a - a + chips_a, chips_a),
        )

    def second_hop(self, parent):
        chips_a, chips_b = self.sizes
        chip = parent // 2
        a, b = chip // chips_b, lax.rem(chip, chips_b)
        return jnp.where(
            self.core == 0,
            lax.rem(self.a - a + chips_a, chips_a),
            lax.rem(self.b - b + chips_b, chips_b),
        )


def parent_of(parents, member):
    return jnp.clip(parents[member], 0, parents.shape[0] - 1)


def routes_kernel(chips, hops, parents, out):
    place = Place(*chips)
    tile = 0
    for hop in range(hops):
        for own in (True, False):
            core = place.core if own else 1 - place.core
            parent = parent_of(parents, place.child(hop, core))
            same = jnp.where(lax.rem(parent, 2) == place.core, 0, 1)
            index = 2 * place.first_hop(parent) + same
            out[pl.ds(tile * SUB, SUB), :] = jnp.full((SUB, LANES), index, jnp.int32)
            tile += 1
    for own in (True, False):
        core = place.core if own else 1 - place.core
        index = place.second_hop(parent_of(parents, place.child(0, core)))
        out[pl.ds(tile * SUB, SUB), :] = jnp.full((SUB, LANES), index, jnp.int32)
        tile += 1


def choose(routes, tile, sources, out):
    index = routes[pl.ds(tile * SUB, SUB), :]
    takes = [index == k for k in range(1, len(sources))]
    for row in range(0, out.shape[0], SUB):
        for lane in range(0, out.shape[1], LANES):
            where = (pl.ds(row, SUB), pl.ds(lane, LANES))
            value = sources[0][where]
            for take, source in zip(takes, sources[1:]):
                value = jnp.where(take, source[where], value)
            out[where] = value


def pick_kernel(hops, routes, *refs):
    held, outs = refs[: 2 * hops], refs[-2 * hops :]
    for tile, out in enumerate(outs):
        choose(routes, tile, held, out)


def settle_kernel(hops, routes, *refs):
    own_half, sibling_half = refs[-2:]
    choose(routes, 2 * hops, refs[:hops], own_half)
    choose(routes, 2 * hops + 1, refs[hops : 2 * hops], sibling_half)


def put_edges(sizes, which, buf, origin, edge_one, edge_two, add=False):
    rows, body, tail = sizes.rows, sizes.body, sizes.tail
    parity = lax.rem(lax.axis_index("domain"), 2)

    def south(edge):
        for f in range(4):
            put(buf, f, origin - body, body, edge, sizes.edge_at(which, f), add)
            put(buf, f, origin - REACH, tail, edge, sizes.tail_at(which, f), add)

    def north(edge):
        for f in range(4):
            put(buf, f, origin + rows, body, edge, sizes.edge_at(which, f), add)
            put(buf, f, origin + rows + body, tail, edge, sizes.tail_at(which, f), add)

    @pl.when(parity == 0)
    def _():
        north(edge_one)
        south(edge_two)

    @pl.when(parity == 1)
    def _():
        south(edge_one)
        north(edge_two)


def score_kernel(sizes, domains, state, edge_one, edge_two, _, out, *bufs):
    rows = sizes.rows
    origin = 16
    total_rows = rows * domains
    domain = lax.axis_index("domain")
    for f in range(4):
        put(bufs[0], f, origin, rows, state.at[f], 0)
    put_edges(sizes, 0, bufs[0], origin, edge_one, edge_two)
    advance(bufs, origin, rows, REACH, domain, domains, total_rows, (3,))
    sub = lax.broadcasted_iota(jnp.int32, (SUB, LANES), 0)
    total = jnp.zeros((SUB, LANES), jnp.float32)
    for row in range(0, rows, SUB):
        line = jnp.zeros((SUB, LANES), jnp.float32)
        for j in range(bufs[0].shape[1]):
            q = bufs[0][3, j, pl.ds(origin + row, SUB), :]
            line = line + q * q
        place = (sub + (row + domain * rows)).astype(jnp.float32)
        total = total + (1.0 + 2.0 * place / (total_rows - 1)) * line
    out[...] = jnp.zeros(out.shape, jnp.float32)
    out[pl.ds(0, SUB), pl.ds(0, LANES)] = total


def total_kernel(cells, score_one, score_two, _, out):
    out[0, 0] = jnp.sum(score_one[...] + score_two[...]) / cells


def final_kernel(
    sizes, domains, own_half, far_half, near_halo, far_halo, pert, edge_one, edge_two, out, last, *bufs
):
    last[...] = jnp.zeros((SUB, LANES), jnp.float32)
    rows, half, extra = sizes.rows, sizes.half, sizes.extra
    origin = 24
    total_rows = rows * domains
    domain = lax.axis_index("domain")
    core = lax.rem(lax.axis_index("member"), 2)
    start = bufs[0]

    def fill(south, north, south_halo, north_halo):
        for f in range(4):
            at, more = sizes.half_at(f), sizes.extra_at(f)
            put(start, f, origin - half, half, south_halo, at)
            put(start, f, origin - half - extra, extra, south_halo, more)
            put(start, f, origin, half, south, at)
            put(start, f, origin + half, half, north, at)
            put(start, f, origin + rows, half, north_halo, at)
            put(start, f, origin + rows + half, extra, north_halo, more)

    @pl.when(core == 0)
    def _():
        fill(own_half, far_half, near_halo, far_halo)

    @pl.when(core == 1)
    def _():
        fill(far_half, own_half, far_halo, near_halo)

    advance(bufs, origin, rows, 2 * REACH, domain, domains, total_rows)
    for f in range(4):
        put(start, f, origin, rows, pert.at[f], 0, add=True)
    put_edges(sizes, 1, start, origin, edge_one, edge_two, add=True)
    advance(bufs, origin, rows, REACH, domain, domains, total_rows)
    for f in range(4):
        for j in range(start.shape[1]):
            out[f, :, pl.ds(j * LANES, LANES)] = start[f, j, pl.ds(origin, rows), :]


def chip_grid(chips):
    b = 1
    while chips % (2 * b) == 0 and (2 * b) * (2 * b) <= chips:
        b *= 2
    return chips // b, b


def on_device(state, perturbation, parents, members, domains):
    state, perturbation = state[0], perturbation[0]
    rows, width = state.shape[1:]
    sizes = Sizes(rows)
    chunks = width // LANES
    chips = chip_grid(members // 2)
    chips_a, chips_b = chips
    hops = max(chips)
    params = pltpu.CompilerParams(vmem_limit_bytes=40 * 2**20)
    half_shape = jax.ShapeDtypeStruct((sizes.half_rows, width), jnp.float32)
    wide_shape = jax.ShapeDtypeStruct((WIDE, width), jnp.float32)
    score_shape = jax.ShapeDtypeStruct((SUB, LANES), jnp.float32)
    edge_shape = jax.ShapeDtypeStruct((sizes.edge_rows, width), jnp.float32)

    def member(a, b, core):
        return ((a % chips_a) * chips_b + b % chips_b) * 2 + core

    everywhere = [(a, b) for a in range(chips_a) for b in range(chips_b)]
    sibling = [(i, i ^ 1) for i in range(members)]

    def same_core(first, k):
        pairs = []
        for a, b in everywhere:
            if k < (chips_b if first else chips_a):
                pairs.append((member(a, b, 0), member(a, b + k, 0) if first else member(a + k, b, 0)))
            if k < (chips_a if first else chips_b):
                pairs.append((member(a, b, 1), member(a + k, b, 1) if first else member(a, b + k, 1)))
        return pairs

    def other_core(k):
        pairs = []
        for a, b in everywhere:
            if k < chips_a:
                pairs.append((member(a, b, 0), member(a + k, b, 1)))
            if k < chips_b:
                pairs.append((member(a, b, 1), member(a, b + k, 0)))
        return pairs

    def flat(m, z):
        return m * domains + z

    levels = range(domains)
    near = members // 2 % 2 == 0

    def matched(partner):
        return [
            (flat(m, z), flat(m, partner(z)) if 0 <= partner(z) < domains else flat(m ^ 1, z))
            for m in range(members)
            for z in levels
        ]

    pair_one = matched(lambda z: z ^ 1)
    pair_two = matched(lambda z: ((z + 1) ^ 1) - 1)
    to_other, to_same = [], []
    for m in range(members):
        core = m % 2
        for z in levels:
            level = z + 1 if core else z - 1
            if 0 <= level < domains:
                to_other.append((flat(m, z), flat(m ^ 1, level)))
                to_same.append((flat(m, z), flat(m, level)))
            else:
                if near:
                    to_other.append((flat(m, z), flat(m ^ 2, z)))
                to_same.append((flat(m, z), flat(m ^ 1, z)))
    both = ("member", "domain")

    def call(kernel, out_shape, in_specs, out_specs, scratch=()):
        return pl.pallas_call(
            kernel,
            out_shape=out_shape,
            in_specs=in_specs,
            out_specs=out_specs,
            scratch_shapes=scratch,
            compiler_params=params,
        )

    mine, other = call(
        functools.partial(pack_kernel, sizes), (half_shape,) * 2, [VMEM], (VMEM,) * 2
    )(state)
    held = [mine, lax.ppermute(other, "member", sibling)]
    for k in range(1, hops):
        held.append(lax.ppermute(mine, "member", same_core(True, k)))
        held.append(lax.ppermute(other, "member", other_core(k)))
    edge_one, edge_two = call(
        functools.partial(edges_kernel, sizes), (edge_shape,) * 2, [VMEM] * 3, (VMEM,) * 2
    )(state, perturbation, held[1])
    edge_one = lax.ppermute(edge_one, both, pair_one)
    edge_two = lax.ppermute(edge_two, both, pair_two)
    routes = call(
        functools.partial(routes_kernel, chips, hops),
        jax.ShapeDtypeStruct(((2 * hops + 2) * SUB, LANES), jnp.int32),
        [SMEM],
        VMEM,
    )(parents)

    picked = call(
        functools.partial(pick_kernel, hops),
        (half_shape,) * (2 * hops),
        [VMEM] * (2 * hops + 1),
        (VMEM,) * (2 * hops),
    )(routes, *held)

    score = call(
        functools.partial(score_kernel, sizes, domains),
        wide_shape,
        [VMEM] * 4,
        VMEM,
        [pltpu.VMEM((4, chunks, rows + 32, LANES), jnp.float32)] * 3,
    )(state, edge_one, edge_two, picked[0])
    scores = [score, jnp.zeros_like(score)]
    bit = 1
    if domains & (domains - 1):
        scores[0] = lax.psum(score, "domain")
    elif domains > 1:
        scores[1] = lax.ppermute(score, "domain", [(z, z ^ 1) for z in range(domains)])
    scores = [part[:SUB, :LANES] for part in scores]

    own, other = [picked[0]], [picked[1]]
    for k in range(1, hops):
        own.append(lax.ppermute(picked[2 * k], "member", same_core(False, k)))
        other.append(lax.ppermute(picked[2 * k + 1], "member", same_core(False, k)))
    own_half, sibling_half = call(
        functools.partial(settle_kernel, hops),
        (half_shape, half_shape),
        [VMEM] * (2 * hops + 1),
        (VMEM,) * 2,
    )(routes, *own, *other)
    near_halo = lax.ppermute(sibling_half, both, to_other)
    far_halo = lax.ppermute(own_half, both, to_same)
    far_half = lax.ppermute(sibling_half, "member", sibling)
    while bit * 2 < domains and domains & (domains - 1) == 0:
        bit *= 2
        score = scores[0] + scores[1]
        pairs = [(z, z ^ bit) for z in range(domains)]
        scores = [score, lax.ppermute(score, "domain", pairs)]
    after, last = call(
        functools.partial(final_kernel, sizes, domains),
        (jax.ShapeDtypeStruct((4, rows, width), jnp.float32), score_shape),
        [VMEM] * 7,
        (VMEM,) * 2,
        [pltpu.VMEM((4, chunks, rows + 48, LANES), jnp.float32)] * 3,
    )(own_half, far_half, near_halo, far_halo, perturbation, edge_one, edge_two)
    score = call(
        functools.partial(total_kernel, rows * domains * width),
        jax.ShapeDtypeStruct((1, 1), jnp.float32),
        [VMEM] * 3,
        SMEM,
    )(*scores, last)
    return after[None], jnp.reshape(score, (1,))


def solution(mesh):
    placed = (P("member", None, "domain", None), P("member", None, "domain", None), P())
    return jax.shard_map(
        functools.partial(
            on_device, members=mesh.shape["member"], domains=mesh.shape["domain"]
        ),
        mesh=mesh,
        in_specs=placed,
        out_specs=(P("member", None, "domain", None), P("member")),
        check_vma=False,
    )
```

```python
import functools

import jax
import jax.numpy as jnp
from jax import lax
from jax.experimental import pallas as pl
from jax.experimental.pallas import tpu as pltpu
from jax.sharding import PartitionSpec as P

STEPS = 3
REACH = 3 * STEPS
WIDE = 16

time_step = 0.1
viscous = 0.05
coriolis = 1.0

LANES = 128
SUB = 8
VMEM = pl.BlockSpec(memory_space=pltpu.VMEM)
SMEM = pl.BlockSpec(memory_space=pltpu.SMEM)


def stage(src, base, dst, first, count, keep, gain, scales, turn, walls, fields):
    scale, scale_out = scales
    chunks = src.shape[1]
    lane = lax.broadcasted_iota(jnp.int32, (SUB, LANES), 1)
    sub = lax.broadcasted_iota(jnp.int32, (SUB, LANES), 0)
    at_last = lane == LANES - 1
    at_first = lane == 0
    step = gain * time_step
    linear = scale_out / scale
    quadratic = -0.5 * step * linear / scale
    diffuse = step * viscous * linear
    middle = (gain - 4.0 * step * viscous) * linear
    slope = 0.5 * step * linear
    keep = keep * scale_out
    turn_first, turn_slope = turn
    for row in range(first, first + count, SUB):

        def load(field, chunk, offset):
            return src[field, chunk, pl.ds(row + offset, SUB), :]

        cells = [[load(f, j, 0) for j in range(chunks)] for f in range(4)]
        to_west = [[pltpu.roll(c, LANES - 1, 1) for c in line] for line in cells]
        to_east = [[pltpu.roll(c, 1, 1) for c in line] for line in cells]
        spin = (turn_first + row * turn_slope) * (step * linear)
        outside = [(sub == at - row) & flag for at, flag in walls if row <= at < row + SUB]
        for j in range(chunks):
            c = [cells[f][j] for f in range(4)]
            n = [load(f, j, 1) for f in range(4)]
            s = [load(f, j, -1) for f in range(4)]
            e = [jnp.where(at_last, to_west[f][(j + 1) % chunks], to_west[f][j]) for f in range(4)]
            w = [jnp.where(at_first, to_east[f][(j - 1) % chunks], to_east[f][j]) for f in range(4)]
            u = c[1] * quadratic
            v = c[2] * quadratic
            by_e, by_w, by_n, by_s = diffuse + u, diffuse - u, diffuse + v, diffuse - v
            for f in fields:
                if f == 0:
                    near = (e[0] + w[0]) + (n[0] + s[0])
                    flux = ((scale + e[0]) * e[1] - (scale + w[0]) * w[1]) + (
                        (scale + n[0]) * n[2] - (scale + s[0]) * s[2]
                    )
                    out = near * diffuse + flux * quadratic
                else:
                    out = (e[f] * by_e + w[f] * by_w) + (n[f] * by_n + s[f] * by_s)
                if f == 1:
                    out = out + (spin * c[2] - (e[0] - w[0]) * slope)
                if f == 2:
                    out = out - (spin * c[1] + (n[0] - s[0]) * slope)
                out = out + (c[f] if abs(middle - 1.0) < 1e-12 else c[f] * middle)
                if keep:
                    kept = base[f, j, pl.ds(row, SUB), :]
                    out = out + (kept if abs(keep - 1.0) < 1e-12 else kept * keep)
                for hide in outside:
                    out = jnp.where(hide, 0.0, out)
                dst[f, j, pl.ds(row, SUB), :] = out


def advance(bufs, origin, rows, reach, domain, domains, total_rows, last_fields=(0, 1, 2, 3)):
    state, one, two = bufs
    sub = lax.broadcasted_iota(jnp.int32, (SUB, LANES), 0)
    slope = 2.0 * coriolis / total_rows
    turn_first = ((sub + (domain * rows - origin)).astype(jnp.float32) + 0.5) * slope - coriolis
    walls = [
        (origin - 1, jnp.full((SUB, LANES), domain, jnp.int32) == 0),
        (origin + rows, jnp.full((SUB, LANES), domain, jnp.int32) == domains - 1),
    ]
    for at, flag in walls:
        for f in range(4):
            for j in range(state.shape[1]):
                line = state[f, j, pl.ds(at, 1), :]
                state[f, j, pl.ds(at, 1), :] = jnp.where(flag[:1], 0.0, line)
    scale_one = 1.0 / (1.0 - 4.0 * time_step * viscous)
    scale_two = 1.0 / 0.75
    thirds = (
        (state, one, 0.0, 1.0, (1.0, scale_one)),
        (one, two, 0.75, 0.25, (scale_one, scale_two)),
        (two, state, 1.0 / 3.0, 2.0 / 3.0, (scale_two, 1.0)),
    )
    for number in range(3 * STEPS):
        src, dst, keep, gain, scales = thirds[number % 3]
        reach -= 1
        first, count = origin - reach, rows + 2 * reach
        fields = range(4) if number < 3 * STEPS - 1 else last_fields
        stage(src, state, dst, first, count, keep, gain, scales, (turn_first, slope), walls, fields)


def put(buf, field, row, count, block, row_from, add=False):
    for j in range(buf.shape[1]):
        piece = block[pl.ds(row_from, count), pl.ds(j * LANES, LANES)]
        if add:
            piece = piece + buf[field, j, pl.ds(row, count), :]
        buf[field, j, pl.ds(row, count), :] = piece


class Sizes:
    def __init__(self, rows):
        self.rows = rows
        self.half = rows // 2
        self.extra = max(0, 2 * REACH - self.half)
        self.half_rows = 4 * (self.half + self.extra)
        self.body = REACH // SUB * SUB
        self.tail = REACH - self.body
        self.edge_rows = 8 * REACH

    def half_at(self, field):
        return field * self.half

    def extra_at(self, field):
        return 4 * self.half + field * self.extra

    def edge_at(self, which, field):
        return (which * 4 + field) * self.body

    def tail_at(self, which, field):
        return 8 * self.body + (which * 4 + field) * self.tail


def pack_kernel(sizes, state, mine, other):
    rows, half, extra = sizes.rows, sizes.half, sizes.extra
    core = lax.rem(lax.axis_index("member"), 2)

    def south_half(out):
        for f in range(4):
            out[pl.ds(sizes.half_at(f), half), :] = state[f, pl.ds(0, half), :]
            out[pl.ds(sizes.extra_at(f), extra), :] = state[f, pl.ds(half, extra), :]

    def north_half(out):
        for f in range(4):
            out[pl.ds(sizes.half_at(f), half), :] = state[f, pl.ds(rows - half, half), :]
            out[pl.ds(sizes.extra_at(f), extra), :] = state[f, pl.ds(rows - half - extra, extra), :]

    @pl.when(core == 0)
    def _():
        south_half(mine)
        north_half(other)

    @pl.when(core == 1)
    def _():
        north_half(mine)
        south_half(other)


def edges_kernel(sizes, state, pert, _, edge_one, edge_two):
    rows, body, tail = sizes.rows, sizes.body, sizes.tail
    parity = lax.rem(lax.axis_index("domain"), 2)

    def south_edge(out):
        for k, a in enumerate((state, pert)):
            for f in range(4):
                out[pl.ds(sizes.edge_at(k, f), body), :] = a[f, pl.ds(0, body), :]
                out[pl.ds(sizes.tail_at(k, f), tail), :] = a[f, pl.ds(body, tail), :]

    def north_edge(out):
        for k, a in enumerate((state, pert)):
            for f in range(4):
                out[pl.ds(sizes.edge_at(k, f), body), :] = a[f, pl.ds(rows - body, body), :]
                out[pl.ds(sizes.tail_at(k, f), tail), :] = a[f, pl.ds(rows - REACH, tail), :]

    @pl.when(parity == 0)
    def _():
        north_edge(edge_one)
        south_edge(edge_two)

    @pl.when(parity == 1)
    def _():
        south_edge(edge_one)
        north_edge(edge_two)


class Place:
    def __init__(self, chips_a, chips_b):
        self.sizes = (chips_a, chips_b)
        member = lax.axis_index("member")
        self.core = lax.rem(member, 2)
        chip = member // 2
        self.a, self.b = chip // chips_b, lax.rem(chip, chips_b)

    def child(self, hop, core):
        chips_a, chips_b = self.sizes
        a = jnp.where(self.core == 0, lax.rem(self.a + hop, chips_a), self.a)
        b = jnp.where(self.core == 0, self.b, lax.rem(self.b + hop, chips_b))
        return (a * chips_b + b) * 2 + core

    def first_hop(self, parent):
        chips_a, chips_b = self.sizes
        chip = parent // 2
        a, b = chip // chips_b, lax.rem(chip, chips_b)
        return jnp.where(
            self.core == 0,
            lax.rem(self.b - b + chips_b, chips_b),
            lax.rem(self.a - a + chips_a, chips_a),
        )


def parent_of(parents, member):
    return jnp.clip(parents[member], 0, parents.shape[0] - 1)


def routes_kernel(chips, hops, parents, out):
    place = Place(*chips)
    tile = 0
    for hop in range(hops):
        for own in (True, False):
            core = 1 - place.core if own else place.core
            parent = parent_of(parents, place.child(hop, core))
            same = jnp.where(lax.rem(parent, 2) == place.core, 0, 1)
            index = 2 * place.first_hop(parent) + same
            out[pl.ds(tile * SUB, SUB), :] = jnp.full((SUB, LANES), index, jnp.int32)
            tile += 1
    for own in (True, False):
        core = place.core if own else 1 - place.core
        index = place.first_hop(parent_of(parents, place.child(0, core)))
        out[pl.ds(tile * SUB, SUB), :] = jnp.full((SUB, LANES), index, jnp.int32)
        tile += 1


def choose(routes, tile, sources, out):
    index = routes[pl.ds(tile * SUB, SUB), :]
    takes = [index == k for k in range(1, len(sources))]
    for row in range(0, out.shape[0], SUB):
        for lane in range(0, out.shape[1], LANES):
            where = (pl.ds(row, SUB), pl.ds(lane, LANES))
            value = sources[0][where]
            for take, source in zip(takes, sources[1:]):
                value = jnp.where(take, source[where], value)
            out[where] = value


def pick_kernel(hops, routes, *refs):
    held, outs = refs[: 2 * hops], refs[-2 * hops :]
    for tile, out in enumerate(outs):
        choose(routes, tile, held, out)


def settle_kernel(hops, routes, *refs):
    own_half, sibling_half = refs[-2:]
    choose(routes, 2 * hops, refs[:hops], own_half)
    choose(routes, 2 * hops + 1, refs[hops : 2 * hops], sibling_half)


def put_edges(sizes, which, buf, origin, edge_one, edge_two, add=False):
    rows, body, tail = sizes.rows, sizes.body, sizes.tail
    parity = lax.rem(lax.axis_index("domain"), 2)

    def south(edge):
        for f in range(4):
            put(buf, f, origin - body, body, edge, sizes.edge_at(which, f), add)
            put(buf, f, origin - REACH, tail, edge, sizes.tail_at(which, f), add)

    def north(edge):
        for f in range(4):
            put(buf, f, origin + rows, body, edge, sizes.edge_at(which, f), add)
            put(buf, f, origin + rows + body, tail, edge, sizes.tail_at(which, f), add)

    @pl.when(parity == 0)
    def _():
        north(edge_one)
        south(edge_two)

    @pl.when(parity == 1)
    def _():
        south(edge_one)
        north(edge_two)


def score_kernel(sizes, domains, state, edge_one, edge_two, _, out, *bufs):
    rows = sizes.rows
    origin = 16
    total_rows = rows * domains
    domain = lax.axis_index("domain")
    for f in range(4):
        put(bufs[0], f, origin, rows, state.at[f], 0)
    put_edges(sizes, 0, bufs[0], origin, edge_one, edge_two)
    advance(bufs, origin, rows, REACH, domain, domains, total_rows, (3,))
    sub = lax.broadcasted_iota(jnp.int32, (SUB, LANES), 0)
    total = jnp.zeros((SUB, LANES), jnp.float32)
    for row in range(0, rows, SUB):
        line = jnp.zeros((SUB, LANES), jnp.float32)
        for j in range(bufs[0].shape[1]):
            q = bufs[0][3, j, pl.ds(origin + row, SUB), :]
            line = line + q * q
        place = (sub + (row + domain * rows)).astype(jnp.float32)
        total = total + (1.0 + 2.0 * place / (total_rows - 1)) * line
    out[...] = jnp.zeros(out.shape, jnp.float32)
    out[pl.ds(0, SUB), pl.ds(0, LANES)] = total


def total_kernel(cells, score_one, score_two, _, out):
    out[0, 0] = jnp.sum(score_one[...] + score_two[...]) / cells


def final_kernel(
    sizes, domains, own_half, far_half, near_halo, far_halo, pert, edge_one, edge_two, out, last, *bufs
):
    last[...] = jnp.zeros((SUB, LANES), jnp.float32)
    rows, half, extra = sizes.rows, sizes.half, sizes.extra
    origin = 24
    total_rows = rows * domains
    domain = lax.axis_index("domain")
    core = lax.rem(lax.axis_index("member"), 2)
    start = bufs[0]

    def fill(south, north, south_halo, north_halo):
        for f in range(4):
            at, more = sizes.half_at(f), sizes.extra_at(f)
            put(start, f, origin - half, half, south_halo, at)
            put(start, f, origin - half - extra, extra, south_halo, more)
            put(start, f, origin, half, south, at)
            put(start, f, origin + half, half, north, at)
            put(start, f, origin + rows, half, north_halo, at)
            put(start, f, origin + rows + half, extra, north_halo, more)

    @pl.when(core == 1)
    def _():
        fill(own_half, far_half, near_halo, far_halo)

    @pl.when(core == 0)
    def _():
        fill(far_half, own_half, far_halo, near_halo)

    advance(bufs, origin, rows, 2 * REACH, domain, domains, total_rows)
    for f in range(4):
        put(start, f, origin, rows, pert.at[f], 0, add=True)
    put_edges(sizes, 1, start, origin, edge_one, edge_two, add=True)
    advance(bufs, origin, rows, REACH, domain, domains, total_rows)
    for f in range(4):
        for j in range(start.shape[1]):
            out[f, :, pl.ds(j * LANES, LANES)] = start[f, j, pl.ds(origin, rows), :]


def chip_grid(chips):
    b = 1
    while chips % (2 * b) == 0 and (2 * b) * (2 * b) <= chips:
        b *= 2
    return chips // b, b


def on_device(state, perturbation, parents, members, domains):
    state, perturbation = state[0], perturbation[0]
    rows, width = state.shape[1:]
    sizes = Sizes(rows)
    chunks = width // LANES
    chips = chip_grid(members // 2)
    chips_a, chips_b = chips
    hops = max(chips)
    params = pltpu.CompilerParams(vmem_limit_bytes=40 * 2**20)
    half_shape = jax.ShapeDtypeStruct((sizes.half_rows, width), jnp.float32)
    wide_shape = jax.ShapeDtypeStruct((WIDE, width), jnp.float32)
    score_shape = jax.ShapeDtypeStruct((SUB, LANES), jnp.float32)
    edge_shape = jax.ShapeDtypeStruct((sizes.edge_rows, width), jnp.float32)

    def member(a, b, core):
        return ((a % chips_a) * chips_b + b % chips_b) * 2 + core

    everywhere = [(a, b) for a in range(chips_a) for b in range(chips_b)]
    sibling = [(i, i ^ 1) for i in range(members)]

    def same_core(first, k):
        pairs = []
        for a, b in everywhere:
            if k < (chips_b if first else chips_a):
                pairs.append((member(a, b, 0), member(a, b + k, 0) if first else member(a + k, b, 0)))
            if k < (chips_a if first else chips_b):
                pairs.append((member(a, b, 1), member(a + k, b, 1) if first else member(a, b + k, 1)))
        return pairs

    def other_core(k):
        pairs = []
        for a, b in everywhere:
            if k < chips_a:
                pairs.append((member(a, b, 0), member(a + k, b, 1)))
            if k < chips_b:
                pairs.append((member(a, b, 1), member(a, b + k, 0)))
        return pairs

    def flat(m, z):
        return m * domains + z

    levels = range(domains)
    near = members // 2 % 2 == 0

    def matched(partner):
        return [
            (flat(m, z), flat(m, partner(z)) if 0 <= partner(z) < domains else flat(m ^ 1, z))
            for m in range(members)
            for z in levels
        ]

    pair_one = matched(lambda z: z ^ 1)
    pair_two = matched(lambda z: ((z + 1) ^ 1) - 1)
    to_other, to_same = [], []
    for m in range(members):
        core = m % 2
        for z in levels:
            level = z - 1 if core else z + 1
            if 0 <= level < domains:
                to_other.append((flat(m, z), flat(m ^ 1, level)))
                to_same.append((flat(m, z), flat(m, level)))
            else:
                if near:
                    to_other.append((flat(m, z), flat(m ^ 2, z)))
                to_same.append((flat(m, z), flat(m ^ 1, z)))
    both = ("member", "domain")

    def call(kernel, out_shape, in_specs, out_specs, scratch=()):
        return pl.pallas_call(
            kernel,
            out_shape=out_shape,
            in_specs=in_specs,
            out_specs=out_specs,
            scratch_shapes=scratch,
            compiler_params=params,
        )

    mine, other = call(
        functools.partial(pack_kernel, sizes), (half_shape,) * 2, [VMEM], (VMEM,) * 2
    )(state)
    held = [mine, lax.ppermute(other, "member", sibling)]
    for k in range(1, hops):
        held.append(lax.ppermute(mine, "member", same_core(True, k)))
        held.append(lax.ppermute(other, "member", other_core(k)))
    edge_one, edge_two = call(
        functools.partial(edges_kernel, sizes), (edge_shape,) * 2, [VMEM] * 3, (VMEM,) * 2
    )(state, perturbation, held[1])
    edge_one = lax.ppermute(edge_one, both, pair_one)
    edge_two = lax.ppermute(edge_two, both, pair_two)
    routes = call(
        functools.partial(routes_kernel, chips, hops),
        jax.ShapeDtypeStruct(((2 * hops + 2) * SUB, LANES), jnp.int32),
        [SMEM],
        VMEM,
    )(parents)

    picked = call(
        functools.partial(pick_kernel, hops),
        (half_shape,) * (2 * hops),
        [VMEM] * (2 * hops + 1),
        (VMEM,) * (2 * hops),
    )(routes, *held)

    score = call(
        functools.partial(score_kernel, sizes, domains),
        wide_shape,
        [VMEM] * 4,
        VMEM,
        [pltpu.VMEM((4, chunks, rows + 32, LANES), jnp.float32)] * 3,
    )(state, edge_one, edge_two, picked[0])
    scores = [score, jnp.zeros_like(score)]
    bit = 1
    if domains & (domains - 1):
        scores[0] = lax.psum(score, "domain")
    elif domains > 1:
        scores[1] = lax.ppermute(score, "domain", [(z, z ^ 1) for z in range(domains)])
    scores = [part[:SUB, :LANES] for part in scores]

    own, other = [], []
    for k in range(1, hops):
        own.append(lax.ppermute(picked[2 * k], "member", other_core(k)))
        other.append(lax.ppermute(picked[2 * k + 1], "member", other_core(k)))
    own.insert(0, lax.ppermute(picked[0], "member", sibling))
    other.insert(0, lax.ppermute(picked[1], "member", sibling))
    own_half, sibling_half = call(
        functools.partial(settle_kernel, hops),
        (half_shape, half_shape),
        [VMEM] * (2 * hops + 1),
        (VMEM,) * 2,
    )(routes, *own, *other)
    near_halo = lax.ppermute(sibling_half, both, to_other)
    far_halo = lax.ppermute(own_half, both, to_same)
    far_half = lax.ppermute(sibling_half, "member", sibling)
    while bit * 2 < domains and domains & (domains - 1) == 0:
        bit *= 2
        score = scores[0] + scores[1]
        pairs = [(z, z ^ bit) for z in range(domains)]
        scores = [score, lax.ppermute(score, "domain", pairs)]
    after, last = call(
        functools.partial(final_kernel, sizes, domains),
        (jax.ShapeDtypeStruct((4, rows, width), jnp.float32), score_shape),
        [VMEM] * 7,
        (VMEM,) * 2,
        [pltpu.VMEM((4, chunks, rows + 48, LANES), jnp.float32)] * 3,
    )(own_half, far_half, near_halo, far_halo, perturbation, edge_one, edge_two)
    score = call(
        functools.partial(total_kernel, rows * domains * width),
        jax.ShapeDtypeStruct((1, 1), jnp.float32),
        [VMEM] * 3,
        SMEM,
    )(*scores, last)
    return after[None], jnp.reshape(score, (1,))


def solution(mesh):
    placed = (P("member", None, "domain", None), P("member", None, "domain", None), P())
    return jax.shard_map(
        functools.partial(
            on_device, members=mesh.shape["member"], domains=mesh.shape["domain"]
        ),
        mesh=mesh,
        in_specs=placed,
        out_specs=(P("member", None, "domain", None), P("member")),
        check_vma=False,
    )
```

```python
import functools

import jax
import jax.numpy as jnp
from jax import lax
from jax.experimental import pallas as pl
from jax.experimental.pallas import tpu as pltpu
from jax.sharding import PartitionSpec as P

STEPS = 3
REACH = 3 * STEPS
WIDE = 16

time_step = 0.1
viscous = 0.05
coriolis = 1.0

LANES = 128
SUB = 8
VMEM = pl.BlockSpec(memory_space=pltpu.VMEM)
SMEM = pl.BlockSpec(memory_space=pltpu.SMEM)


def stage(src, base, dst, first, count, keep, gain, scales, turn, walls, fields):
    scale, scale_out = scales
    chunks = src.shape[1]
    lane = lax.broadcasted_iota(jnp.int32, (SUB, LANES), 1)
    sub = lax.broadcasted_iota(jnp.int32, (SUB, LANES), 0)
    at_last = lane == LANES - 1
    at_first = lane == 0
    step = gain * time_step
    linear = scale_out / scale
    quadratic = -0.5 * step * linear / scale
    diffuse = step * viscous * linear
    middle = (gain - 4.0 * step * viscous) * linear
    slope = 0.5 * step * linear
    keep = keep * scale_out
    turn_first, turn_slope = turn
    for row in range(first, first + count, SUB):

        def load(field, chunk, offset):
            return src[field, chunk, pl.ds(row + offset, SUB), :]

        spin = (turn_first + row * turn_slope) * (step * linear)
        outside = [(sub == at - row) & flag for at, flag in walls if row <= at < row + SUB]
        for j in range(chunks):
            c = [load(f, j, 0) for f in range(4)]
            n = [load(f, j, 1) for f in range(4)]
            s = [load(f, j, -1) for f in range(4)]
            after = [load(f, (j + 1) % chunks, 0) for f in range(4)]
            before = [load(f, (j - 1) % chunks, 0) for f in range(4)]
            e = [pltpu.roll(jnp.where(at_first, after[f], c[f]), LANES - 1, 1) for f in range(4)]
            w = [pltpu.roll(jnp.where(at_last, before[f], c[f]), 1, 1) for f in range(4)]
            u = c[1] * quadratic
            v = c[2] * quadratic
            by_e, by_w, by_n, by_s = diffuse + u, diffuse - u, diffuse + v, diffuse - v
            for f in fields:
                if f == 0:
                    near = (e[0] + w[0]) + (n[0] + s[0])
                    flux = ((scale + e[0]) * e[1] - (scale + w[0]) * w[1]) + (
                        (scale + n[0]) * n[2] - (scale + s[0]) * s[2]
                    )
                    out = near * diffuse + flux * quadratic
                else:
                    out = (e[f] * by_e + w[f] * by_w) + (n[f] * by_n + s[f] * by_s)
                if f == 1:
                    out = out + (spin * c[2] - (e[0] - w[0]) * slope)
                if f == 2:
                    out = out - (spin * c[1] + (n[0] - s[0]) * slope)
                out = out + (c[f] if abs(middle - 1.0) < 1e-12 else c[f] * middle)
                if keep:
                    kept = base[f, j, pl.ds(row, SUB), :]
                    out = out + (kept if abs(keep - 1.0) < 1e-12 else kept * keep)
                for hide in outside:
                    out = jnp.where(hide, 0.0, out)
                dst[f, j, pl.ds(row, SUB), :] = out


def advance(bufs, origin, rows, reach, domain, domains, total_rows, last_fields=(0, 1, 2, 3)):
    state, one, two = bufs
    sub = lax.broadcasted_iota(jnp.int32, (SUB, LANES), 0)
    slope = 2.0 * coriolis / total_rows
    turn_first = ((sub + (domain * rows - origin)).astype(jnp.float32) + 0.5) * slope - coriolis
    walls = [
        (origin - 1, jnp.full((SUB, LANES), domain, jnp.int32) == 0),
        (origin + rows, jnp.full((SUB, LANES), domain, jnp.int32) == domains - 1),
    ]
    for at, flag in walls:
        for f in range(4):
            for j in range(state.shape[1]):
                line = state[f, j, pl.ds(at, 1), :]
                state[f, j, pl.ds(at, 1), :] = jnp.where(flag[:1], 0.0, line)
    scale_one = 1.0 / (1.0 - 4.0 * time_step * viscous)
    scale_two = 1.0 / 0.75
    thirds = (
        (state, one, 0.0, 1.0, (1.0, scale_one)),
        (one, two, 0.75, 0.25, (scale_one, scale_two)),
        (two, state, 1.0 / 3.0, 2.0 / 3.0, (scale_two, 1.0)),
    )
    for number in range(3 * STEPS):
        src, dst, keep, gain, scales = thirds[number % 3]
        reach -= 1
        first, count = origin - reach, rows + 2 * reach
        fields = range(4) if number < 3 * STEPS - 1 else last_fields
        stage(src, state, dst, first, count, keep, gain, scales, (turn_first, slope), walls, fields)


def put(buf, field, row, count, block, row_from, add=False):
    for j in range(buf.shape[1]):
        piece = block[pl.ds(row_from, count), pl.ds(j * LANES, LANES)]
        if add:
            piece = piece + buf[field, j, pl.ds(row, count), :]
        buf[field, j, pl.ds(row, count), :] = piece


class Sizes:
    def __init__(self, rows):
        self.rows = rows
        self.half = rows // 2
        self.extra = max(0, 2 * REACH - self.half)
        self.half_rows = 4 * (self.half + self.extra)
        self.body = REACH // SUB * SUB
        self.tail = REACH - self.body
        self.edge_rows = 8 * REACH

    def half_at(self, field):
        return field * self.half

    def extra_at(self, field):
        return 4 * self.half + field * self.extra

    def edge_at(self, which, field):
        return (which * 4 + field) * self.body

    def tail_at(self, which, field):
        return 8 * self.body + (which * 4 + field) * self.tail


def pack_kernel(sizes, state, mine, other):
    rows, half, extra = sizes.rows, sizes.half, sizes.extra
    core = lax.rem(lax.axis_index("member"), 2)

    def south_half(out):
        for f in range(4):
            out[pl.ds(sizes.half_at(f), half), :] = state[f, pl.ds(0, half), :]
            out[pl.ds(sizes.extra_at(f), extra), :] = state[f, pl.ds(half, extra), :]

    def north_half(out):
        for f in range(4):
            out[pl.ds(sizes.half_at(f), half), :] = state[f, pl.ds(rows - half, half), :]
            out[pl.ds(sizes.extra_at(f), extra), :] = state[f, pl.ds(rows - half - extra, extra), :]

    @pl.when(core == 0)
    def _():
        south_half(mine)
        north_half(other)

    @pl.when(core == 1)
    def _():
        north_half(mine)
        south_half(other)


def edges_kernel(sizes, state, pert, _, edge_one, edge_two):
    rows, body, tail = sizes.rows, sizes.body, sizes.tail
    parity = lax.rem(lax.axis_index("domain"), 2)

    def south_edge(out):
        for k, a in enumerate((state, pert)):
            for f in range(4):
                out[pl.ds(sizes.edge_at(k, f), body), :] = a[f, pl.ds(0, body), :]
                out[pl.ds(sizes.tail_at(k, f), tail), :] = a[f, pl.ds(body, tail), :]

    def north_edge(out):
        for k, a in enumerate((state, pert)):
            for f in range(4):
                out[pl.ds(sizes.edge_at(k, f), body), :] = a[f, pl.ds(rows - body, body), :]
                out[pl.ds(sizes.tail_at(k, f), tail), :] = a[f, pl.ds(rows - REACH, tail), :]

    @pl.when(parity == 0)
    def _():
        north_edge(edge_one)
        south_edge(edge_two)

    @pl.when(parity == 1)
    def _():
        south_edge(edge_one)
        north_edge(edge_two)


class Place:
    def __init__(self, chips_a, chips_b):
        self.sizes = (chips_a, chips_b)
        member = lax.axis_index("member")
        self.core = lax.rem(member, 2)
        chip = member // 2
        self.a, self.b = chip // chips_b, lax.rem(chip, chips_b)

    def child(self, hop, core):
        chips_a, chips_b = self.sizes
        a = jnp.where(self.core == 0, lax.rem(self.a + hop, chips_a), self.a)
        b = jnp.where(self.core == 0, self.b, lax.rem(self.b + hop, chips_b))
        return (a * chips_b + b) * 2 + core

    def first_hop(self, parent):
        chips_a, chips_b = self.sizes
        chip = parent // 2
        a, b = chip // chips_b, lax.rem(chip, chips_b)
        return jnp.where(
            self.core == 0,
            lax.rem(self.b - b + chips_b, chips_b),
            lax.rem(self.a - a + chips_a, chips_a),
        )


def parent_of(parents, member):
    return jnp.clip(parents[member], 0, parents.shape[0] - 1)


def routes_kernel(chips, hops, parents, out):
    place = Place(*chips)
    tile = 0
    for hop in range(hops):
        for own in (True, False):
            core = 1 - place.core if own else place.core
            parent = parent_of(parents, place.child(hop, core))
            same = jnp.where(lax.rem(parent, 2) == place.core, 0, 1)
            index = 2 * place.first_hop(parent) + same
            out[pl.ds(tile * SUB, SUB), :] = jnp.full((SUB, LANES), index, jnp.int32)
            tile += 1
    for own in (True, False):
        core = place.core if own else 1 - place.core
        index = place.first_hop(parent_of(parents, place.child(0, core)))
        out[pl.ds(tile * SUB, SUB), :] = jnp.full((SUB, LANES), index, jnp.int32)
        tile += 1


def choose(routes, tile, sources, out):
    index = routes[pl.ds(tile * SUB, SUB), :]
    takes = [index == k for k in range(1, len(sources))]
    for row in range(0, out.shape[0], SUB):
        for lane in range(0, out.shape[1], LANES):
            where = (pl.ds(row, SUB), pl.ds(lane, LANES))
            value = sources[0][where]
            for take, source in zip(takes, sources[1:]):
                value = jnp.where(take, source[where], value)
            out[where] = value


def pick_kernel(hops, routes, *refs):
    held, outs = refs[: 2 * hops], refs[-2 * hops :]
    for tile, out in enumerate(outs):
        choose(routes, tile, held, out)


def settle_kernel(hops, routes, *refs):
    own_half, sibling_half = refs[-2:]
    choose(routes, 2 * hops, refs[:hops], own_half)
    choose(routes, 2 * hops + 1, refs[hops : 2 * hops], sibling_half)


def put_edges(sizes, which, buf, origin, edge_one, edge_two, add=False):
    rows, body, tail = sizes.rows, sizes.body, sizes.tail
    parity = lax.rem(lax.axis_index("domain"), 2)

    def south(edge):
        for f in range(4):
            put(buf, f, origin - body, body, edge, sizes.edge_at(which, f), add)
            put(buf, f, origin - REACH, tail, edge, sizes.tail_at(which, f), add)

    def north(edge):
        for f in range(4):
            put(buf, f, origin + rows, body, edge, sizes.edge_at(which, f), add)
            put(buf, f, origin + rows + body, tail, edge, sizes.tail_at(which, f), add)

    @pl.when(parity == 0)
    def _():
        north(edge_one)
        south(edge_two)

    @pl.when(parity == 1)
    def _():
        south(edge_one)
        north(edge_two)


def score_kernel(sizes, domains, state, edge_one, edge_two, _, out, *bufs):
    rows = sizes.rows
    origin = 16
    total_rows = rows * domains
    domain = lax.axis_index("domain")
    for f in range(4):
        put(bufs[0], f, origin, rows, state.at[f], 0)
    put_edges(sizes, 0, bufs[0], origin, edge_one, edge_two)
    advance(bufs, origin, rows, REACH, domain, domains, total_rows, (3,))
    sub = lax.broadcasted_iota(jnp.int32, (SUB, LANES), 0)
    total = jnp.zeros((SUB, LANES), jnp.float32)
    for row in range(0, rows, SUB):
        line = jnp.zeros((SUB, LANES), jnp.float32)
        for j in range(bufs[0].shape[1]):
            q = bufs[0][3, j, pl.ds(origin + row, SUB), :]
            line = line + q * q
        place = (sub + (row + domain * rows)).astype(jnp.float32)
        total = total + (1.0 + 2.0 * place / (total_rows - 1)) * line
    out[...] = jnp.zeros(out.shape, jnp.float32)
    out[pl.ds(0, SUB), pl.ds(0, LANES)] = total


def total_kernel(cells, score_one, score_two, _, out):
    out[0, 0] = jnp.sum(score_one[...] + score_two[...]) / cells


def final_kernel(
    sizes, domains, own_half, far_half, near_halo, far_halo, pert, edge_one, edge_two, out, last, *bufs
):
    last[...] = jnp.zeros((SUB, LANES), jnp.float32)
    rows, half, extra = sizes.rows, sizes.half, sizes.extra
    origin = 24
    total_rows = rows * domains
    domain = lax.axis_index("domain")
    core = lax.rem(lax.axis_index("member"), 2)
    start = bufs[0]

    def fill(south, north, south_halo, north_halo):
        for f in range(4):
            at, more = sizes.half_at(f), sizes.extra_at(f)
            put(start, f, origin - half, half, south_halo, at)
            put(start, f, origin - half - extra, extra, south_halo, more)
            put(start, f, origin, half, south, at)
            put(start, f, origin + half, half, north, at)
            put(start, f, origin + rows, half, north_halo, at)
            put(start, f, origin + rows + half, extra, north_halo, more)

    @pl.when(core == 1)
    def _():
        fill(own_half, far_half, near_halo, far_halo)

    @pl.when(core == 0)
    def _():
        fill(far_half, own_half, far_halo, near_halo)

    advance(bufs, origin, rows, 2 * REACH, domain, domains, total_rows)
    for f in range(4):
        put(start, f, origin, rows, pert.at[f], 0, add=True)
    put_edges(sizes, 1, start, origin, edge_one, edge_two, add=True)
    advance(bufs, origin, rows, REACH, domain, domains, total_rows)
    for f in range(4):
        for j in range(start.shape[1]):
            out[f, :, pl.ds(j * LANES, LANES)] = start[f, j, pl.ds(origin, rows), :]


def chip_grid(chips):
    b = 1
    while chips % (2 * b) == 0 and (2 * b) * (2 * b) <= chips:
        b *= 2
    return chips // b, b


def on_device(state, perturbation, parents, members, domains):
    state, perturbation = state[0], perturbation[0]
    rows, width = state.shape[1:]
    sizes = Sizes(rows)
    chunks = width // LANES
    chips = chip_grid(members // 2)
    chips_a, chips_b = chips
    hops = max(chips)
    params = pltpu.CompilerParams(vmem_limit_bytes=40 * 2**20)
    half_shape = jax.ShapeDtypeStruct((sizes.half_rows, width), jnp.float32)
    wide_shape = jax.ShapeDtypeStruct((WIDE, width), jnp.float32)
    score_shape = jax.ShapeDtypeStruct((SUB, LANES), jnp.float32)
    edge_shape = jax.ShapeDtypeStruct((sizes.edge_rows, width), jnp.float32)

    def member(a, b, core):
        return ((a % chips_a) * chips_b + b % chips_b) * 2 + core

    everywhere = [(a, b) for a in range(chips_a) for b in range(chips_b)]
    sibling = [(i, i ^ 1) for i in range(members)]

    def same_core(first, k):
        pairs = []
        for a, b in everywhere:
            if k < (chips_b if first else chips_a):
                pairs.append((member(a, b, 0), member(a, b + k, 0) if first else member(a + k, b, 0)))
            if k < (chips_a if first else chips_b):
                pairs.append((member(a, b, 1), member(a + k, b, 1) if first else member(a, b + k, 1)))
        return pairs

    def other_core(k):
        pairs = []
        for a, b in everywhere:
            if k < chips_a:
                pairs.append((member(a, b, 0), member(a + k, b, 1)))
            if k < chips_b:
                pairs.append((member(a, b, 1), member(a, b + k, 0)))
        return pairs

    def flat(m, z):
        return m * domains + z

    levels = range(domains)
    near = members // 2 % 2 == 0

    def matched(partner):
        return [
            (flat(m, z), flat(m, partner(z)) if 0 <= partner(z) < domains else flat(m ^ 1, z))
            for m in range(members)
            for z in levels
        ]

    pair_one = matched(lambda z: z ^ 1)
    pair_two = matched(lambda z: ((z + 1) ^ 1) - 1)
    to_other, to_same = [], []
    for m in range(members):
        core = m % 2
        for z in levels:
            level = z - 1 if core else z + 1
            if 0 <= level < domains:
                to_other.append((flat(m, z), flat(m ^ 1, level)))
                to_same.append((flat(m, z), flat(m, level)))
            else:
                if near:
                    to_other.append((flat(m, z), flat(m ^ 2, z)))
                to_same.append((flat(m, z), flat(m ^ 1, z)))
    both = ("member", "domain")

    def call(kernel, out_shape, in_specs, out_specs, scratch=()):
        return pl.pallas_call(
            kernel,
            out_shape=out_shape,
            in_specs=in_specs,
            out_specs=out_specs,
            scratch_shapes=scratch,
            compiler_params=params,
        )

    mine, other = call(
        functools.partial(pack_kernel, sizes), (half_shape,) * 2, [VMEM], (VMEM,) * 2
    )(state)
    held = [mine, lax.ppermute(other, "member", sibling)]
    for k in range(1, hops):
        held.append(lax.ppermute(mine, "member", same_core(True, k)))
        held.append(lax.ppermute(other, "member", other_core(k)))
    edge_one, edge_two = call(
        functools.partial(edges_kernel, sizes), (edge_shape,) * 2, [VMEM] * 3, (VMEM,) * 2
    )(state, perturbation, held[1])
    edge_one = lax.ppermute(edge_one, both, pair_one)
    edge_two = lax.ppermute(edge_two, both, pair_two)
    routes = call(
        functools.partial(routes_kernel, chips, hops),
        jax.ShapeDtypeStruct(((2 * hops + 2) * SUB, LANES), jnp.int32),
        [SMEM],
        VMEM,
    )(parents)

    picked = call(
        functools.partial(pick_kernel, hops),
        (half_shape,) * (2 * hops),
        [VMEM] * (2 * hops + 1),
        (VMEM,) * (2 * hops),
    )(routes, *held)

    score = call(
        functools.partial(score_kernel, sizes, domains),
        wide_shape,
        [VMEM] * 4,
        VMEM,
        [pltpu.VMEM((4, chunks, rows + 32, LANES), jnp.float32)] * 3,
    )(state, edge_one, edge_two, picked[0])
    scores = [score, jnp.zeros_like(score)]
    bit = 1
    if domains & (domains - 1):
        scores[0] = lax.psum(score, "domain")
    elif domains > 1:
        scores[1] = lax.ppermute(score, "domain", [(z, z ^ 1) for z in range(domains)])
    scores = [part[:SUB, :LANES] for part in scores]

    own, other = [], []
    for k in range(1, hops):
        own.append(lax.ppermute(picked[2 * k], "member", other_core(k)))
        other.append(lax.ppermute(picked[2 * k + 1], "member", other_core(k)))
    own.insert(0, lax.ppermute(picked[0], "member", sibling))
    other.insert(0, lax.ppermute(picked[1], "member", sibling))
    own_half, sibling_half = call(
        functools.partial(settle_kernel, hops),
        (half_shape, half_shape),
        [VMEM] * (2 * hops + 1),
        (VMEM,) * 2,
    )(routes, *own, *other)
    near_halo = lax.ppermute(sibling_half, both, to_other)
    far_halo = lax.ppermute(own_half, both, to_same)
    far_half = lax.ppermute(sibling_half, "member", sibling)
    while bit * 2 < domains and domains & (domains - 1) == 0:
        bit *= 2
        score = scores[0] + scores[1]
        pairs = [(z, z ^ bit) for z in range(domains)]
        scores = [score, lax.ppermute(score, "domain", pairs)]
    after, last = call(
        functools.partial(final_kernel, sizes, domains),
        (jax.ShapeDtypeStruct((4, rows, width), jnp.float32), score_shape),
        [VMEM] * 7,
        (VMEM,) * 2,
        [pltpu.VMEM((4, chunks, rows + 48, LANES), jnp.float32)] * 3,
    )(own_half, far_half, near_halo, far_halo, perturbation, edge_one, edge_two)
    score = call(
        functools.partial(total_kernel, rows * domains * width),
        jax.ShapeDtypeStruct((1, 1), jnp.float32),
        [VMEM] * 3,
        SMEM,
    )(*scores, last)
    return after[None], jnp.reshape(score, (1,))


def solution(mesh):
    placed = (P("member", None, "domain", None), P("member", None, "domain", None), P())
    return jax.shard_map(
        functools.partial(
            on_device, members=mesh.shape["member"], domains=mesh.shape["domain"]
        ),
        mesh=mesh,
        in_specs=placed,
        out_specs=(P("member", None, "domain", None), P("member")),
        check_vma=False,
    )
```

```python
import functools

import jax
import jax.numpy as jnp
from jax import lax
from jax.experimental import pallas as pl
from jax.experimental.pallas import tpu as pltpu
from jax.sharding import PartitionSpec as P

STEPS = 3
REACH = 3 * STEPS
WIDE = 16

time_step = 0.1
viscous = 0.05
coriolis = 1.0

LANES = 128
SUB = 8
VMEM = pl.BlockSpec(memory_space=pltpu.VMEM)
SMEM = pl.BlockSpec(memory_space=pltpu.SMEM)


def stage(src, base, dst, first, count, keep, gain, scales, turn, walls, fields):
    scale, scale_out = scales
    chunks = src.shape[1]
    lane = lax.broadcasted_iota(jnp.int32, (SUB, LANES), 1)
    sub = lax.broadcasted_iota(jnp.int32, (SUB, LANES), 0)
    at_last = lane == LANES - 1
    at_first = lane == 0
    step = gain * time_step
    linear = scale_out / scale
    quadratic = -0.5 * step * linear / scale
    diffuse = step * viscous * linear
    middle = (gain - 4.0 * step * viscous) * linear
    slope = 0.5 * step * linear
    keep = keep * scale_out
    turn_first, turn_slope = turn
    for row in range(first, first + count, SUB):

        def load(field, chunk, offset):
            return src[field, chunk, pl.ds(row + offset, SUB), :]

        spin = (turn_first + row * turn_slope) * (step * linear)
        outside = [(sub == at - row) & flag for at, flag in walls if row <= at < row + SUB]
        for j in range(chunks):
            c = [load(f, j, 0) for f in range(4)]
            n = [load(f, j, 1) for f in range(4)]
            s = [load(f, j, -1) for f in range(4)]
            after = [load(f, (j + 1) % chunks, 0) for f in range(4)]
            before = [load(f, (j - 1) % chunks, 0) for f in range(4)]
            e = [pltpu.roll(jnp.where(at_first, after[f], c[f]), LANES - 1, 1) for f in range(4)]
            w = [pltpu.roll(jnp.where(at_last, before[f], c[f]), 1, 1) for f in range(4)]
            u = c[1] * quadratic
            v = c[2] * quadratic
            by_e, by_w, by_n, by_s = diffuse + u, diffuse - u, diffuse + v, diffuse - v
            for f in fields:
                if f == 0:
                    near = (e[0] + w[0]) + (n[0] + s[0])
                    flux = ((scale + e[0]) * e[1] - (scale + w[0]) * w[1]) + (
                        (scale + n[0]) * n[2] - (scale + s[0]) * s[2]
                    )
                    out = near * diffuse + flux * quadratic
                else:
                    out = (e[f] * by_e + w[f] * by_w) + (n[f] * by_n + s[f] * by_s)
                if f == 1:
                    out = out + (spin * c[2] - (e[0] - w[0]) * slope)
                if f == 2:
                    out = out - (spin * c[1] + (n[0] - s[0]) * slope)
                out = out + (c[f] if abs(middle - 1.0) < 1e-12 else c[f] * middle)
                if keep:
                    kept = base[f, j, pl.ds(row, SUB), :]
                    out = out + (kept if abs(keep - 1.0) < 1e-12 else kept * keep)
                for hide in outside:
                    out = jnp.where(hide, 0.0, out)
                dst[f, j, pl.ds(row, SUB), :] = out


def advance(bufs, origin, rows, reach, domain, domains, total_rows, last_fields=(0, 1, 2, 3)):
    state, one, two = bufs
    sub = lax.broadcasted_iota(jnp.int32, (SUB, LANES), 0)
    slope = 2.0 * coriolis / total_rows
    turn_first = ((sub + (domain * rows - origin)).astype(jnp.float32) + 0.5) * slope - coriolis
    walls = [
        (origin - 1, jnp.full((SUB, LANES), domain, jnp.int32) == 0),
        (origin + rows, jnp.full((SUB, LANES), domain, jnp.int32) == domains - 1),
    ]
    for at, flag in walls:
        for f in range(4):
            for j in range(state.shape[1]):
                line = state[f, j, pl.ds(at, 1), :]
                state[f, j, pl.ds(at, 1), :] = jnp.where(flag[:1], 0.0, line)
    scale_one = 1.0 / (1.0 - 4.0 * time_step * viscous)
    scale_two = 1.0 / 0.75
    thirds = (
        (state, one, 0.0, 1.0, (1.0, scale_one)),
        (one, two, 0.75, 0.25, (scale_one, scale_two)),
        (two, state, 1.0 / 3.0, 2.0 / 3.0, (scale_two, 1.0)),
    )
    for number in range(3 * STEPS):
        src, dst, keep, gain, scales = thirds[number % 3]
        reach -= 1
        first, count = origin - reach, rows + 2 * reach
        fields = range(4) if number < 3 * STEPS - 1 else last_fields
        stage(src, state, dst, first, count, keep, gain, scales, (turn_first, slope), walls, fields)


def put(buf, field, row, count, block, row_from, add=False):
    for j in range(buf.shape[1]):
        piece = block[pl.ds(row_from, count), pl.ds(j * LANES, LANES)]
        if add:
            piece = piece + buf[field, j, pl.ds(row, count), :]
        buf[field, j, pl.ds(row, count), :] = piece


class Sizes:
    def __init__(self, rows):
        self.rows = rows
        self.half = rows // 2
        self.extra = max(0, 2 * REACH - self.half)
        self.half_rows = 4 * (self.half + self.extra)
        self.body = REACH // SUB * SUB
        self.tail = REACH - self.body
        self.edge_rows = 8 * REACH

    def half_at(self, field):
        return field * self.half

    def extra_at(self, field):
        return 4 * self.half + field * self.extra

    def edge_at(self, which, field):
        return (which * 4 + field) * self.body

    def tail_at(self, which, field):
        return 8 * self.body + (which * 4 + field) * self.tail


def pack_kernel(sizes, state, mine, other):
    rows, half, extra = sizes.rows, sizes.half, sizes.extra
    core = lax.rem(lax.axis_index("member"), 2)

    def south_half(out):
        for f in range(4):
            out[pl.ds(sizes.half_at(f), half), :] = state[f, pl.ds(0, half), :]
            out[pl.ds(sizes.extra_at(f), extra), :] = state[f, pl.ds(half, extra), :]

    def north_half(out):
        for f in range(4):
            out[pl.ds(sizes.half_at(f), half), :] = state[f, pl.ds(rows - half, half), :]
            out[pl.ds(sizes.extra_at(f), extra), :] = state[f, pl.ds(rows - half - extra, extra), :]

    @pl.when(core == 0)
    def _():
        south_half(mine)
        north_half(other)

    @pl.when(core == 1)
    def _():
        north_half(mine)
        south_half(other)


def edges_kernel(sizes, state, pert, _, edge_one, edge_two):
    rows, body, tail = sizes.rows, sizes.body, sizes.tail
    parity = lax.rem(lax.axis_index("domain"), 2)

    def south_edge(out):
        for k, a in enumerate((state, pert)):
            for f in range(4):
                out[pl.ds(sizes.edge_at(k, f), body), :] = a[f, pl.ds(0, body), :]
                out[pl.ds(sizes.tail_at(k, f), tail), :] = a[f, pl.ds(body, tail), :]

    def north_edge(out):
        for k, a in enumerate((state, pert)):
            for f in range(4):
                out[pl.ds(sizes.edge_at(k, f), body), :] = a[f, pl.ds(rows - body, body), :]
                out[pl.ds(sizes.tail_at(k, f), tail), :] = a[f, pl.ds(rows - REACH, tail), :]

    @pl.when(parity == 0)
    def _():
        north_edge(edge_one)
        south_edge(edge_two)

    @pl.when(parity == 1)
    def _():
        south_edge(edge_one)
        north_edge(edge_two)


class Place:
    def __init__(self, chips_a, chips_b):
        self.sizes = (chips_a, chips_b)
        member = lax.axis_index("member")
        self.core = lax.rem(member, 2)
        chip = member // 2
        self.a, self.b = chip // chips_b, lax.rem(chip, chips_b)

    def child(self, hop, core):
        chips_a, chips_b = self.sizes
        a = jnp.where(self.core == 0, lax.rem(self.a + hop, chips_a), self.a)
        b = jnp.where(self.core == 0, self.b, lax.rem(self.b + hop, chips_b))
        return (a * chips_b + b) * 2 + core

    def first_hop(self, parent):
        chips_a, chips_b = self.sizes
        chip = parent // 2
        a, b = chip // chips_b, lax.rem(chip, chips_b)
        return jnp.where(
            self.core == 0,
            lax.rem(self.b - b + chips_b, chips_b),
            lax.rem(self.a - a + chips_a, chips_a),
        )


def parent_of(parents, member):
    return jnp.clip(parents[member], 0, parents.shape[0] - 1)


def routes_kernel(chips, hops, parents, out):
    place = Place(*chips)
    tile = 0
    for hop in range(hops):
        for own in (True, False):
            core = 1 - place.core if own else place.core
            parent = parent_of(parents, place.child(hop, core))
            same = jnp.where(lax.rem(parent, 2) == place.core, 0, 1)
            index = 2 * place.first_hop(parent) + same
            out[pl.ds(tile * SUB, SUB), :] = jnp.full((SUB, LANES), index, jnp.int32)
            tile += 1
    for own in (True, False):
        core = place.core if own else 1 - place.core
        index = place.first_hop(parent_of(parents, place.child(0, core)))
        out[pl.ds(tile * SUB, SUB), :] = jnp.full((SUB, LANES), index, jnp.int32)
        tile += 1


def choose(routes, tile, sources, out):
    index = routes[pl.ds(tile * SUB, SUB), :]
    takes = [index == k for k in range(1, len(sources))]
    for row in range(0, out.shape[0], SUB):
        for lane in range(0, out.shape[1], LANES):
            where = (pl.ds(row, SUB), pl.ds(lane, LANES))
            value = sources[0][where]
            for take, source in zip(takes, sources[1:]):
                value = jnp.where(take, source[where], value)
            out[where] = value


def pick_kernel(first, hops, routes, *refs):
    held, outs = refs[: 2 * hops], refs[2 * hops :]
    if first == 0:
        outs = outs[1:]
    for tile, out in enumerate(outs, 2 * first):
        choose(routes, tile, held, out)


def settle_kernel(hops, which, routes, *refs):
    choose(routes, 2 * hops + which, refs[:hops], refs[-1])


def put_edges(sizes, which, buf, origin, edge_one, edge_two, add=False):
    rows, body, tail = sizes.rows, sizes.body, sizes.tail
    parity = lax.rem(lax.axis_index("domain"), 2)

    def south(edge):
        for f in range(4):
            put(buf, f, origin - body, body, edge, sizes.edge_at(which, f), add)
            put(buf, f, origin - REACH, tail, edge, sizes.tail_at(which, f), add)

    def north(edge):
        for f in range(4):
            put(buf, f, origin + rows, body, edge, sizes.edge_at(which, f), add)
            put(buf, f, origin + rows + body, tail, edge, sizes.tail_at(which, f), add)

    @pl.when(parity == 0)
    def _():
        north(edge_one)
        south(edge_two)

    @pl.when(parity == 1)
    def _():
        south(edge_one)
        north(edge_two)


def score_kernel(sizes, domains, state, edge_one, edge_two, _, out, *bufs):
    rows = sizes.rows
    origin = 16
    total_rows = rows * domains
    domain = lax.axis_index("domain")
    for f in range(4):
        put(bufs[0], f, origin, rows, state.at[f], 0)
    put_edges(sizes, 0, bufs[0], origin, edge_one, edge_two)
    advance(bufs, origin, rows, REACH, domain, domains, total_rows, (3,))
    sub = lax.broadcasted_iota(jnp.int32, (SUB, LANES), 0)
    total = jnp.zeros((SUB, LANES), jnp.float32)
    for row in range(0, rows, SUB):
        line = jnp.zeros((SUB, LANES), jnp.float32)
        for j in range(bufs[0].shape[1]):
            q = bufs[0][3, j, pl.ds(origin + row, SUB), :]
            line = line + q * q
        place = (sub + (row + domain * rows)).astype(jnp.float32)
        total = total + (1.0 + 2.0 * place / (total_rows - 1)) * line
    out[...] = jnp.zeros(out.shape, jnp.float32)
    out[pl.ds(0, SUB), pl.ds(0, LANES)] = total


def late_kernel(half, _, out):
    out[...] = half[...]


def total_kernel(cells, score_one, score_two, _, out):
    summed = jnp.sum(score_one[...] + score_two[...], axis=0, keepdims=True)
    out[...] = jnp.sum(summed, axis=1, keepdims=True) / cells


def final_kernel(
    sizes, domains, own_half, far_half, near_halo, far_halo, pert, edge_one, edge_two, out, last, *bufs
):
    last[...] = jnp.zeros((SUB, LANES), jnp.float32)
    rows, half, extra = sizes.rows, sizes.half, sizes.extra
    origin = 24
    total_rows = rows * domains
    domain = lax.axis_index("domain")
    core = lax.rem(lax.axis_index("member"), 2)
    start = bufs[0]

    def fill(south, north, south_halo, north_halo):
        for f in range(4):
            at, more = sizes.half_at(f), sizes.extra_at(f)
            put(start, f, origin - half, half, south_halo, at)
            put(start, f, origin - half - extra, extra, south_halo, more)
            put(start, f, origin, half, south, at)
            put(start, f, origin + half, half, north, at)
            put(start, f, origin + rows, half, north_halo, at)
            put(start, f, origin + rows + half, extra, north_halo, more)

    @pl.when(core == 1)
    def _():
        fill(own_half, far_half, near_halo, far_halo)

    @pl.when(core == 0)
    def _():
        fill(far_half, own_half, far_halo, near_halo)

    advance(bufs, origin, rows, 2 * REACH, domain, domains, total_rows)
    for f in range(4):
        put(start, f, origin, rows, pert.at[f], 0, add=True)
    put_edges(sizes, 1, start, origin, edge_one, edge_two, add=True)
    advance(bufs, origin, rows, REACH, domain, domains, total_rows)
    for f in range(4):
        for j in range(start.shape[1]):
            out[f, :, pl.ds(j * LANES, LANES)] = start[f, j, pl.ds(origin, rows), :]


def chip_grid(chips):
    b = 1
    while chips % (2 * b) == 0 and (2 * b) * (2 * b) <= chips:
        b *= 2
    return chips // b, b


def on_device(state, perturbation, parents, members, domains):
    state, perturbation = state[0], perturbation[0]
    rows, width = state.shape[1:]
    sizes = Sizes(rows)
    chunks = width // LANES
    chips = chip_grid(members // 2)
    chips_a, chips_b = chips
    hops = max(chips)
    params = pltpu.CompilerParams(vmem_limit_bytes=40 * 2**20)
    half_shape = jax.ShapeDtypeStruct((sizes.half_rows, width), jnp.float32)
    wide_shape = jax.ShapeDtypeStruct((WIDE, width), jnp.float32)
    score_shape = jax.ShapeDtypeStruct((SUB, LANES), jnp.float32)
    edge_shape = jax.ShapeDtypeStruct((sizes.edge_rows, width), jnp.float32)

    def member(a, b, core):
        return ((a % chips_a) * chips_b + b % chips_b) * 2 + core

    everywhere = [(a, b) for a in range(chips_a) for b in range(chips_b)]
    sibling = [(i, i ^ 1) for i in range(members)]

    def same_core(first, k):
        pairs = []
        for a, b in everywhere:
            if k < (chips_b if first else chips_a):
                pairs.append((member(a, b, 0), member(a, b + k, 0) if first else member(a + k, b, 0)))
            if k < (chips_a if first else chips_b):
                pairs.append((member(a, b, 1), member(a + k, b, 1) if first else member(a, b + k, 1)))
        return pairs

    def other_core(k):
        pairs = []
        for a, b in everywhere:
            if k < chips_a:
                pairs.append((member(a, b, 0), member(a + k, b, 1)))
            if k < chips_b:
                pairs.append((member(a, b, 1), member(a, b + k, 0)))
        return pairs

    def flat(m, z):
        return m * domains + z

    levels = range(domains)
    near = members // 2 % 2 == 0

    def matched(partner):
        return [
            (flat(m, z), flat(m, partner(z)) if 0 <= partner(z) < domains else flat(m ^ 1, z))
            for m in range(members)
            for z in levels
        ]

    pair_one = matched(lambda z: z ^ 1)
    pair_two = matched(lambda z: ((z + 1) ^ 1) - 1)
    to_other, to_same = [], []
    for m in range(members):
        core = m % 2
        for z in levels:
            level = z - 1 if core else z + 1
            if 0 <= level < domains:
                to_other.append((flat(m, z), flat(m ^ 1, level)))
                to_same.append((flat(m, z), flat(m, level)))
            else:
                if near:
                    to_other.append((flat(m, z), flat(m ^ 2, z)))
                to_same.append((flat(m, z), flat(m ^ 1, z)))
    both = ("member", "domain")

    def call(kernel, out_shape, in_specs, out_specs, scratch=()):
        return pl.pallas_call(
            kernel,
            out_shape=out_shape,
            in_specs=in_specs,
            out_specs=out_specs,
            scratch_shapes=scratch,
            compiler_params=params,
        )

    mine, other = call(
        functools.partial(pack_kernel, sizes), (half_shape,) * 2, [VMEM], (VMEM,) * 2
    )(state)
    held = [mine, lax.ppermute(other, "member", sibling)]
    for k in range(1, hops):
        held.append(lax.ppermute(mine, "member", same_core(True, k)))
        held.append(lax.ppermute(other, "member", other_core(k)))
    edge_one, edge_two = call(
        functools.partial(edges_kernel, sizes), (edge_shape,) * 2, [VMEM] * 3, (VMEM,) * 2
    )(state, perturbation, held[1])
    edge_one = lax.ppermute(edge_one, both, pair_one)
    edge_two = lax.ppermute(edge_two, both, pair_two)
    routes = call(
        functools.partial(routes_kernel, chips, hops),
        jax.ShapeDtypeStruct(((2 * hops + 2) * SUB, LANES), jnp.int32),
        [SMEM],
        VMEM,
    )(parents)

    picked = call(
        functools.partial(pick_kernel, 1, hops),
        (half_shape,) * (2 * hops - 2),
        [VMEM] * (2 * hops + 1),
        (VMEM,) * (2 * hops - 2),
    )(routes, *held)
    stay = call(
        functools.partial(pick_kernel, 0, hops),
        (half_shape,) * 2,
        [VMEM] * (2 * hops + 2),
        (VMEM,) * 2,
    )(routes, *held, picked[0])

    score = call(
        functools.partial(score_kernel, sizes, domains),
        wide_shape,
        [VMEM] * 4,
        VMEM,
        [pltpu.VMEM((4, chunks, rows + 32, LANES), jnp.float32)] * 3,
    )(state, edge_one, edge_two, stay[0])
    scores = [score, jnp.zeros_like(score)]
    bit = 1
    if domains & (domains - 1):
        scores[0] = lax.psum(score, "domain")
    elif domains > 1:
        scores[1] = lax.ppermute(score, "domain", [(z, z ^ 1) for z in range(domains)])
    scores = [part[:SUB, :LANES] for part in scores]

    own = [lax.ppermute(stay[0], "member", sibling)]
    other = [lax.ppermute(stay[1], "member", sibling)]
    for k in range(hops - 1):
        own.append(lax.ppermute(picked[2 * k], "member", other_core(k + 1)))
        other.append(lax.ppermute(picked[2 * k + 1], "member", other_core(k + 1)))
    own_half, sibling_half = [
        call(
            functools.partial(settle_kernel, hops, which),
            half_shape,
            [VMEM] * (hops + 1),
            VMEM,
        )(routes, *sources)
        for which, sources in enumerate((own, other))
    ]
    near_halo = lax.ppermute(sibling_half, both, to_other)
    far_halo = lax.ppermute(own_half, both, to_same)
    (held_back,) = call(late_kernel, (half_shape,), [VMEM] * 2, (VMEM,))(sibling_half, scores[1])
    far_half = lax.ppermute(held_back, "member", sibling)
    while bit * 2 < domains and domains & (domains - 1) == 0:
        bit *= 2
        score = scores[0] + scores[1]
        pairs = [(z, z ^ bit) for z in range(domains)]
        scores = [score, lax.ppermute(score, "domain", pairs)]
    after, last = call(
        functools.partial(final_kernel, sizes, domains),
        (jax.ShapeDtypeStruct((4, rows, width), jnp.float32), score_shape),
        [VMEM] * 7,
        (VMEM,) * 2,
        [pltpu.VMEM((4, chunks, rows + 48, LANES), jnp.float32)] * 3,
    )(own_half, far_half, near_halo, far_halo, perturbation, edge_one, edge_two)
    score = call(
        functools.partial(total_kernel, rows * domains * width),
        jax.ShapeDtypeStruct((1, 1), jnp.float32),
        [VMEM] * 3,
        VMEM,
    )(*scores, last)
    return after[None], jnp.reshape(score, (1,))


def solution(mesh):
    placed = (P("member", None, "domain", None), P("member", None, "domain", None), P())
    return jax.shard_map(
        functools.partial(
            on_device, members=mesh.shape["member"], domains=mesh.shape["domain"]
        ),
        mesh=mesh,
        in_specs=placed,
        out_specs=(P("member", None, "domain", None), P("member")),
        check_vma=False,
    )
```

```python
import functools

import jax
import jax.numpy as jnp
from jax import lax
from jax.experimental import pallas as pl
from jax.experimental.pallas import tpu as pltpu
from jax.sharding import PartitionSpec as P

STEPS = 3
REACH = 3 * STEPS
WIDE = 16

time_step = 0.1
viscous = 0.05
coriolis = 1.0

LANES = 128
SUB = 8
VMEM = pl.BlockSpec(memory_space=pltpu.VMEM)
SMEM = pl.BlockSpec(memory_space=pltpu.SMEM)


def stage(src, base, dst, first, count, keep, gain, scales, turn, walls, fields):
    scale, scale_out = scales
    chunks = src.shape[1]
    lane = lax.broadcasted_iota(jnp.int32, (SUB, LANES), 1)
    sub = lax.broadcasted_iota(jnp.int32, (SUB, LANES), 0)
    at_last = lane == LANES - 1
    at_first = lane == 0
    step = gain * time_step
    linear = scale_out / scale
    quadratic = -0.5 * step * linear / scale
    diffuse = step * viscous * linear
    middle = (gain - 4.0 * step * viscous) * linear
    slope = 0.5 * step * linear
    keep = keep * scale_out
    turn_first, turn_slope = turn
    for row in range(first, first + count, SUB):

        def load(field, chunk, offset):
            return src[field, chunk, pl.ds(row + offset, SUB), :]

        spin = (turn_first + row * turn_slope) * (step * linear)
        outside = [(sub == at - row) & flag for at, flag in walls if row <= at < row + SUB]
        for j in range(chunks):
            c = [load(f, j, 0) for f in range(4)]
            n = [load(f, j, 1) for f in range(4)]
            s = [load(f, j, -1) for f in range(4)]
            after = [load(f, (j + 1) % chunks, 0) for f in range(4)]
            before = [load(f, (j - 1) % chunks, 0) for f in range(4)]
            e = [pltpu.roll(jnp.where(at_first, after[f], c[f]), LANES - 1, 1) for f in range(4)]
            w = [pltpu.roll(jnp.where(at_last, before[f], c[f]), 1, 1) for f in range(4)]
            u = c[1] * quadratic
            v = c[2] * quadratic
            by_e, by_w, by_n, by_s = diffuse + u, diffuse - u, diffuse + v, diffuse - v
            for f in fields:
                if f == 0:
                    near = (e[0] + w[0]) + (n[0] + s[0])
                    flux = ((scale + e[0]) * e[1] - (scale + w[0]) * w[1]) + (
                        (scale + n[0]) * n[2] - (scale + s[0]) * s[2]
                    )
                    out = near * diffuse + flux * quadratic
                else:
                    out = (e[f] * by_e + w[f] * by_w) + (n[f] * by_n + s[f] * by_s)
                if f == 1:
                    out = out + (spin * c[2] - (e[0] - w[0]) * slope)
                if f == 2:
                    out = out - (spin * c[1] + (n[0] - s[0]) * slope)
                out = out + (c[f] if abs(middle - 1.0) < 1e-12 else c[f] * middle)
                if keep:
                    kept = base[f, j, pl.ds(row, SUB), :]
                    out = out + (kept if abs(keep - 1.0) < 1e-12 else kept * keep)
                for hide in outside:
                    out = jnp.where(hide, 0.0, out)
                dst[f, j, pl.ds(row, SUB), :] = out


def advance(bufs, origin, rows, reach, domain, domains, total_rows, last_fields=(0, 1, 2, 3)):
    state, one, two = bufs
    sub = lax.broadcasted_iota(jnp.int32, (SUB, LANES), 0)
    slope = 2.0 * coriolis / total_rows
    turn_first = ((sub + (domain * rows - origin)).astype(jnp.float32) + 0.5) * slope - coriolis
    walls = [
        (origin - 1, jnp.full((SUB, LANES), domain, jnp.int32) == 0),
        (origin + rows, jnp.full((SUB, LANES), domain, jnp.int32) == domains - 1),
    ]
    for at, flag in walls:
        for f in range(4):
            for j in range(state.shape[1]):
                line = state[f, j, pl.ds(at, 1), :]
                state[f, j, pl.ds(at, 1), :] = jnp.where(flag[:1], 0.0, line)
    scale_one = 1.0 / (1.0 - 4.0 * time_step * viscous)
    scale_two = 1.0 / 0.75
    thirds = (
        (state, one, 0.0, 1.0, (1.0, scale_one)),
        (one, two, 0.75, 0.25, (scale_one, scale_two)),
        (two, state, 1.0 / 3.0, 2.0 / 3.0, (scale_two, 1.0)),
    )
    for number in range(3 * STEPS):
        src, dst, keep, gain, scales = thirds[number % 3]
        reach -= 1
        first, count = origin - reach, rows + 2 * reach
        fields = range(4) if number < 3 * STEPS - 1 else last_fields
        if number == 3 * STEPS - 2 and last_fields == (3,):
            fields = (1, 2, 3)
        stage(src, state, dst, first, count, keep, gain, scales, (turn_first, slope), walls, fields)


def put(buf, field, row, count, block, row_from, add=False):
    for j in range(buf.shape[1]):
        piece = block[pl.ds(row_from, count), pl.ds(j * LANES, LANES)]
        if add:
            piece = piece + buf[field, j, pl.ds(row, count), :]
        buf[field, j, pl.ds(row, count), :] = piece


class Sizes:
    def __init__(self, rows):
        self.rows = rows
        self.half = rows // 2
        self.extra = max(0, 2 * REACH - self.half)
        self.half_rows = 4 * (self.half + self.extra)
        self.body = REACH // SUB * SUB
        self.tail = REACH - self.body
        self.edge_rows = 8 * REACH

    def half_at(self, field):
        return field * self.half

    def extra_at(self, field):
        return 4 * self.half + field * self.extra

    def edge_at(self, which, field):
        return (which * 4 + field) * self.body

    def tail_at(self, which, field):
        return 8 * self.body + (which * 4 + field) * self.tail


def pack_kernel(sizes, state, mine, other):
    rows, half, extra = sizes.rows, sizes.half, sizes.extra
    core = lax.rem(lax.axis_index("member"), 2)

    def south_half(out):
        for f in range(4):
            out[pl.ds(sizes.half_at(f), half), :] = state[f, pl.ds(0, half), :]
            out[pl.ds(sizes.extra_at(f), extra), :] = state[f, pl.ds(half, extra), :]

    def north_half(out):
        for f in range(4):
            out[pl.ds(sizes.half_at(f), half), :] = state[f, pl.ds(rows - half, half), :]
            out[pl.ds(sizes.extra_at(f), extra), :] = state[f, pl.ds(rows - half - extra, extra), :]

    @pl.when(core == 0)
    def _():
        south_half(mine)
        north_half(other)

    @pl.when(core == 1)
    def _():
        north_half(mine)
        south_half(other)


def edges_kernel(sizes, state, pert, _, edge_one, edge_two):
    rows, body, tail = sizes.rows, sizes.body, sizes.tail
    parity = lax.rem(lax.axis_index("domain"), 2)

    def south_edge(out):
        for k, a in enumerate((state, pert)):
            for f in range(4):
                out[pl.ds(sizes.edge_at(k, f), body), :] = a[f, pl.ds(0, body), :]
                out[pl.ds(sizes.tail_at(k, f), tail), :] = a[f, pl.ds(body, tail), :]

    def north_edge(out):
        for k, a in enumerate((state, pert)):
            for f in range(4):
                out[pl.ds(sizes.edge_at(k, f), body), :] = a[f, pl.ds(rows - body, body), :]
                out[pl.ds(sizes.tail_at(k, f), tail), :] = a[f, pl.ds(rows - REACH, tail), :]

    @pl.when(parity == 0)
    def _():
        north_edge(edge_one)
        south_edge(edge_two)

    @pl.when(parity == 1)
    def _():
        south_edge(edge_one)
        north_edge(edge_two)


class Place:
    def __init__(self, chips_a, chips_b):
        self.sizes = (chips_a, chips_b)
        member = lax.axis_index("member")
        self.core = lax.rem(member, 2)
        chip = member // 2
        self.a, self.b = chip // chips_b, lax.rem(chip, chips_b)

    def child(self, hop, core):
        chips_a, chips_b = self.sizes
        a = jnp.where(self.core == 0, lax.rem(self.a + hop, chips_a), self.a)
        b = jnp.where(self.core == 0, self.b, lax.rem(self.b + hop, chips_b))
        return (a * chips_b + b) * 2 + core

    def first_hop(self, parent):
        chips_a, chips_b = self.sizes
        chip = parent // 2
        a, b = chip // chips_b, lax.rem(chip, chips_b)
        return jnp.where(
            self.core == 0,
            lax.rem(self.b - b + chips_b, chips_b),
            lax.rem(self.a - a + chips_a, chips_a),
        )


def parent_of(parents, member):
    return jnp.clip(parents[member], 0, parents.shape[0] - 1)


def routes_kernel(chips, hops, parents, out):
    place = Place(*chips)
    tile = 0
    for hop in range(hops):
        for own in (True, False):
            core = 1 - place.core if own else place.core
            parent = parent_of(parents, place.child(hop, core))
            same = jnp.where(lax.rem(parent, 2) == place.core, 0, 1)
            index = 2 * place.first_hop(parent) + same
            out[pl.ds(tile * SUB, SUB), :] = jnp.full((SUB, LANES), index, jnp.int32)
            tile += 1
    for own in (True, False):
        core = place.core if own else 1 - place.core
        index = place.first_hop(parent_of(parents, place.child(0, core)))
        out[pl.ds(tile * SUB, SUB), :] = jnp.full((SUB, LANES), index, jnp.int32)
        tile += 1


def choose(routes, tile, sources, out):
    index = routes[pl.ds(tile * SUB, SUB), :]
    takes = [index == k for k in range(1, len(sources))]
    for row in range(0, out.shape[0], SUB):
        for lane in range(0, out.shape[1], LANES):
            where = (pl.ds(row, SUB), pl.ds(lane, LANES))
            value = sources[0][where]
            for take, source in zip(takes, sources[1:]):
                value = jnp.where(take, source[where], value)
            out[where] = value


def pick_kernel(first, hops, routes, *refs):
    held, outs = refs[: 2 * hops], refs[2 * hops :]
    if first == 0:
        outs = outs[1:]
    for tile, out in enumerate(outs, 2 * first):
        choose(routes, tile, held, out)


def settle_kernel(hops, which, routes, *refs):
    choose(routes, 2 * hops + which, refs[:hops], refs[-1])


def put_edges(sizes, which, buf, origin, edge_one, edge_two, add=False):
    rows, body, tail = sizes.rows, sizes.body, sizes.tail
    parity = lax.rem(lax.axis_index("domain"), 2)

    def south(edge):
        for f in range(4):
            put(buf, f, origin - body, body, edge, sizes.edge_at(which, f), add)
            put(buf, f, origin - REACH, tail, edge, sizes.tail_at(which, f), add)

    def north(edge):
        for f in range(4):
            put(buf, f, origin + rows, body, edge, sizes.edge_at(which, f), add)
            put(buf, f, origin + rows + body, tail, edge, sizes.tail_at(which, f), add)

    @pl.when(parity == 0)
    def _():
        north(edge_one)
        south(edge_two)

    @pl.when(parity == 1)
    def _():
        south(edge_one)
        north(edge_two)


def score_kernel(sizes, domains, state, edge_one, edge_two, _, out, *bufs):
    rows = sizes.rows
    origin = 16
    total_rows = rows * domains
    domain = lax.axis_index("domain")
    for f in range(4):
        put(bufs[0], f, origin, rows, state.at[f], 0)
    put_edges(sizes, 0, bufs[0], origin, edge_one, edge_two)
    advance(bufs, origin, rows, REACH, domain, domains, total_rows, (3,))
    sub = lax.broadcasted_iota(jnp.int32, (SUB, LANES), 0)
    total = jnp.zeros((SUB, LANES), jnp.float32)
    for row in range(0, rows, SUB):
        line = jnp.zeros((SUB, LANES), jnp.float32)
        for j in range(bufs[0].shape[1]):
            q = bufs[0][3, j, pl.ds(origin + row, SUB), :]
            line = line + q * q
        place = (sub + (row + domain * rows)).astype(jnp.float32)
        total = total + (1.0 + 2.0 * place / (total_rows - 1)) * line
    out[...] = jnp.zeros(out.shape, jnp.float32)
    out[pl.ds(0, SUB), pl.ds(0, LANES)] = total


def late_kernel(half, _, out):
    out[...] = half[...]


def total_kernel(cells, score_one, score_two, _, out):
    summed = jnp.sum(score_one[...] + score_two[...], axis=0, keepdims=True)
    out[...] = jnp.sum(summed, axis=1, keepdims=True) / cells


def final_kernel(
    sizes, domains, own_half, far_half, near_halo, far_halo, pert, edge_one, edge_two, out, last, *bufs
):
    last[...] = jnp.zeros((SUB, LANES), jnp.float32)
    rows, half, extra = sizes.rows, sizes.half, sizes.extra
    origin = 24
    total_rows = rows * domains
    domain = lax.axis_index("domain")
    core = lax.rem(lax.axis_index("member"), 2)
    start = bufs[0]

    def fill(south, north, south_halo, north_halo):
        for f in range(4):
            at, more = sizes.half_at(f), sizes.extra_at(f)
            put(start, f, origin - half, half, south_halo, at)
            put(start, f, origin - half - extra, extra, south_halo, more)
            put(start, f, origin, half, south, at)
            put(start, f, origin + half, half, north, at)
            put(start, f, origin + rows, half, north_halo, at)
            put(start, f, origin + rows + half, extra, north_halo, more)

    @pl.when(core == 1)
    def _():
        fill(own_half, far_half, near_halo, far_halo)

    @pl.when(core == 0)
    def _():
        fill(far_half, own_half, far_halo, near_halo)

    advance(bufs, origin, rows, 2 * REACH, domain, domains, total_rows)
    for f in range(4):
        put(start, f, origin, rows, pert.at[f], 0, add=True)
    put_edges(sizes, 1, start, origin, edge_one, edge_two, add=True)
    advance(bufs, origin, rows, REACH, domain, domains, total_rows)
    for f in range(4):
        for j in range(start.shape[1]):
            out[f, :, pl.ds(j * LANES, LANES)] = start[f, j, pl.ds(origin, rows), :]


def chip_grid(chips):
    b = 1
    while chips % (2 * b) == 0 and (2 * b) * (2 * b) <= chips:
        b *= 2
    return chips // b, b


def on_device(state, perturbation, parents, members, domains):
    state, perturbation = state[0], perturbation[0]
    rows, width = state.shape[1:]
    sizes = Sizes(rows)
    chunks = width // LANES
    chips = chip_grid(members // 2)
    chips_a, chips_b = chips
    hops = max(chips)
    params = pltpu.CompilerParams(vmem_limit_bytes=40 * 2**20)
    half_shape = jax.ShapeDtypeStruct((sizes.half_rows, width), jnp.float32)
    wide_shape = jax.ShapeDtypeStruct((WIDE, width), jnp.float32)
    score_shape = jax.ShapeDtypeStruct((SUB, LANES), jnp.float32)
    edge_shape = jax.ShapeDtypeStruct((sizes.edge_rows, width), jnp.float32)

    def member(a, b, core):
        return ((a % chips_a) * chips_b + b % chips_b) * 2 + core

    everywhere = [(a, b) for a in range(chips_a) for b in range(chips_b)]
    sibling = [(i, i ^ 1) for i in range(members)]

    def same_core(first, k):
        pairs = []
        for a, b in everywhere:
            if k < (chips_b if first else chips_a):
                pairs.append((member(a, b, 0), member(a, b + k, 0) if first else member(a + k, b, 0)))
            if k < (chips_a if first else chips_b):
                pairs.append((member(a, b, 1), member(a + k, b, 1) if first else member(a, b + k, 1)))
        return pairs

    def other_core(k):
        pairs = []
        for a, b in everywhere:
            if k < chips_a:
                pairs.append((member(a, b, 0), member(a + k, b, 1)))
            if k < chips_b:
                pairs.append((member(a, b, 1), member(a, b + k, 0)))
        return pairs

    def flat(m, z):
        return m * domains + z

    levels = range(domains)
    near = members // 2 % 2 == 0

    def matched(partner):
        return [
            (flat(m, z), flat(m, partner(z)) if 0 <= partner(z) < domains else flat(m ^ 1, z))
            for m in range(members)
            for z in levels
        ]

    pair_one = matched(lambda z: z ^ 1)
    pair_two = matched(lambda z: ((z + 1) ^ 1) - 1)
    to_other, to_same = [], []
    for m in range(members):
        core = m % 2
        for z in levels:
            level = z - 1 if core else z + 1
            if 0 <= level < domains:
                to_other.append((flat(m, z), flat(m ^ 1, level)))
                to_same.append((flat(m, z), flat(m, level)))
            else:
                if near:
                    to_other.append((flat(m, z), flat(m ^ 2, z)))
                to_same.append((flat(m, z), flat(m ^ 1, z)))
    both = ("member", "domain")

    def call(kernel, out_shape, in_specs, out_specs, scratch=()):
        return pl.pallas_call(
            kernel,
            out_shape=out_shape,
            in_specs=in_specs,
            out_specs=out_specs,
            scratch_shapes=scratch,
            compiler_params=params,
        )

    mine, other = call(
        functools.partial(pack_kernel, sizes), (half_shape,) * 2, [VMEM], (VMEM,) * 2
    )(state)
    held = [mine, lax.ppermute(other, "member", sibling)]
    for k in range(1, hops):
        held.append(lax.ppermute(mine, "member", same_core(True, k)))
        held.append(lax.ppermute(other, "member", other_core(k)))
    edge_one, edge_two = call(
        functools.partial(edges_kernel, sizes), (edge_shape,) * 2, [VMEM] * 3, (VMEM,) * 2
    )(state, perturbation, held[1])
    edge_one = lax.ppermute(edge_one, both, pair_one)
    edge_two = lax.ppermute(edge_two, both, pair_two)
    routes = call(
        functools.partial(routes_kernel, chips, hops),
        jax.ShapeDtypeStruct(((2 * hops + 2) * SUB, LANES), jnp.int32),
        [SMEM],
        VMEM,
    )(parents)

    picked = call(
        functools.partial(pick_kernel, 1, hops),
        (half_shape,) * (2 * hops - 2),
        [VMEM] * (2 * hops + 1),
        (VMEM,) * (2 * hops - 2),
    )(routes, *held)
    stay = call(
        functools.partial(pick_kernel, 0, hops),
        (half_shape,) * 2,
        [VMEM] * (2 * hops + 2),
        (VMEM,) * 2,
    )(routes, *held, picked[0])

    score = call(
        functools.partial(score_kernel, sizes, domains),
        wide_shape,
        [VMEM] * 4,
        VMEM,
        [pltpu.VMEM((4, chunks, rows + 32, LANES), jnp.float32)] * 3,
    )(state, edge_one, edge_two, stay[0])
    scores = [score, jnp.zeros_like(score)]
    bit = 1
    if domains & (domains - 1):
        scores[0] = lax.psum(score, "domain")
    elif domains > 1:
        scores[1] = lax.ppermute(score, "domain", [(z, z ^ 1) for z in range(domains)])
    scores = [part[:SUB, :LANES] for part in scores]

    own = [lax.ppermute(stay[0], "member", sibling)]
    other = [lax.ppermute(stay[1], "member", sibling)]
    for k in range(hops - 1):
        own.append(lax.ppermute(picked[2 * k], "member", other_core(k + 1)))
        other.append(lax.ppermute(picked[2 * k + 1], "member", other_core(k + 1)))
    own_half, sibling_half = [
        call(
            functools.partial(settle_kernel, hops, which),
            half_shape,
            [VMEM] * (hops + 1),
            VMEM,
        )(routes, *sources)
        for which, sources in enumerate((own, other))
    ]
    far_halo = lax.ppermute(own_half, both, to_same)
    near_halo = lax.ppermute(sibling_half, both, to_other)
    (held_back,) = call(late_kernel, (half_shape,), [VMEM] * 2, (VMEM,))(sibling_half, scores[1])
    far_half = lax.ppermute(held_back, "member", sibling)
    while bit * 2 < domains and domains & (domains - 1) == 0:
        bit *= 2
        score = scores[0] + scores[1]
        pairs = [(z, z ^ bit) for z in range(domains)]
        scores = [score, lax.ppermute(score, "domain", pairs)]
    after, last = call(
        functools.partial(final_kernel, sizes, domains),
        (jax.ShapeDtypeStruct((4, rows, width), jnp.float32), score_shape),
        [VMEM] * 7,
        (VMEM,) * 2,
        [pltpu.VMEM((4, chunks, rows + 48, LANES), jnp.float32)] * 3,
    )(own_half, far_half, near_halo, far_halo, perturbation, edge_one, edge_two)
    score = call(
        functools.partial(total_kernel, rows * domains * width),
        jax.ShapeDtypeStruct((1, 1), jnp.float32),
        [VMEM] * 3,
        VMEM,
    )(*scores, last)
    return after[None], jnp.reshape(score, (1,))


def solution(mesh):
    placed = (P("member", None, "domain", None), P("member", None, "domain", None), P())
    return jax.shard_map(
        functools.partial(
            on_device, members=mesh.shape["member"], domains=mesh.shape["domain"]
        ),
        mesh=mesh,
        in_specs=placed,
        out_specs=(P("member", None, "domain", None), P("member")),
        check_vma=False,
    )
```
